512 devices in a mesh: img: 32 (over y, z_lo, core), rows: 16 (over z_hi, x).
Axes of the slice: x: 4, y: 8, z: 8 (z_hi: 4, z_lo: 2; z = z_hi * 2 + z_lo), core: 2. Of those that a mesh axis runs over, the one named last changes fastest.
Arguments:
- center_mid: bfloat16 [32, 64, 32, 512], P('img', 'rows'), may hold values from -6 to 6
- radius_mid: bfloat16 [32, 64, 32, 512], P('img', 'rows'), may hold values from 0.049804688 to 1.5
- conv_weight: bfloat16 [512, 3, 3, 512], P('img'), may hold values from -0.09375 to 0.09375
- center_upstream: bfloat16 [32, 64, 32, 512], P('img', 'rows'), may hold values from -6 to 6
- radius_upstream: bfloat16 [32, 64, 32, 512], P('img', 'rows'), may hold values from -6 to 6
Outputs:
- center_mid_grad: bfloat16 [32, 64, 32, 512], P('img', 'rows')
- radius_mid_grad: bfloat16 [32, 64, 32, 512], P('img', 'rows')
- weight_grad: float32 [512, 3, 3, 512], P('img', None, None, 'rows')
The draws below stay inside these ranges and needn't reach their ends.
All inputs are finite; a program needn't handle non-finite values.
Results may differ from the reference program's by a relative error of at most 0.0055.
Values may be sent and summed in bfloat16 or wider, within the bound.
A program may use at most 64 MiB of HBM per device.

```python
import math
import jax
import jax.numpy as jnp
from jax import lax

C = 512
COLS = 32
BATCH = 32
HEIGHT = 64


def spiked(drawn, stream_key, source, target, shards_of, factor):
    def block_of(axis_at):
        return (jnp.arange(drawn.shape[axis_at]) // (drawn.shape[axis_at] // shards_of)).reshape((-1,) + (1,) * (drawn.ndim - 1 - axis_at))

    near = jax.random.permutation(stream_key, shards_of)[block_of(target)]
    second = (block_of(target) + shards_of // 2) % shards_of
    return jnp.where((block_of(source) == near) | (block_of(source) == second), factor * drawn, drawn)


def block_scale(rng, extent, split, smallest, largest):
    def one(dim, blocks):
        heights = jax.random.uniform(jax.random.fold_in(jax.random.fold_in(rng, 6), dim), (blocks,), jnp.float32, smallest / len(split), largest / len(split))
        return jnp.repeat(jnp.exp(heights), extent[dim] // blocks).reshape((-1,) + (1,) * (len(extent) - dim - 1))

    level = one(*split[0])
    for cut in split[1:]:
        level = level * one(*cut)
    return level


def normal_values(own_key, shape, width, reach, shards=(), held_as=jnp.bfloat16):
    drawn = width * jax.random.normal(own_key, shape, jnp.float32)
    if shards:
        drawn = drawn * block_scale(own_key, shape, shards, -0.22, 0.18)
    return jnp.clip(drawn, -reach, reach).astype(held_as)


def gaussian_with(rng, dims, scale, most, cuts, heavy, dtype=jnp.bfloat16):
    values = scale * jax.random.normal(rng, dims, jnp.float32)
    if cuts:
        values = values * block_scale(rng, dims, cuts, -0.22, 0.18)
    return jnp.clip(spiked(values, jax.random.fold_in(rng, 3), *heavy), -most, most).astype(dtype)


def setup_inputs(seed: int = 0) -> dict:
    arg_keys = jax.random.split(jax.random.key(seed), 6)
    center_mid = normal_values(arg_keys[0], (BATCH, HEIGHT, COLS, C), 1.0, 6.0, ((0, 32), (1, 16)))
    radius_mid = jnp.clip(jnp.exp(math.log(1.5) - 3.4051113 * jax.random.uniform(arg_keys[1], (BATCH, HEIGHT, COLS, C), jnp.float32) ** block_scale(arg_keys[1], (BATCH, HEIGHT, COLS, C), ((0, 32), (1, 16)), -0.2, 0.2)), 0.049804688, 1.5).astype(jnp.bfloat16)
    conv_weight = normal_values(arg_keys[2], (C, 3, 3, C), (9 * C) ** -0.5, 0.09375, ((0, 32),))
    center_upstream = gaussian_with(arg_keys[3], (BATCH, HEIGHT, COLS, C), 1.0, 6.0, ((0, 32), (1, 16)), (1, 3, 16, 2.0))
    radius_upstream = gaussian_with(arg_keys[4], (BATCH, HEIGHT, COLS, C), 1.0, 6.0, ((0, 32), (1, 16)), (1, 3, 16, 2.0))
    return dict(center_mid=center_mid, radius_mid=radius_mid, conv_weight=conv_weight, center_upstream=center_upstream, radius_upstream=radius_upstream)


def back_data(upstream, weight):
    row_count = upstream.shape[1]
    col_count = upstream.shape[2]
    padded = jnp.pad(upstream.astype(jnp.float32), ((0, 0), (1, 1), (1, 1), (0, 0)))
    weight_wide = weight.astype(jnp.float32)
    total = jnp.zeros(upstream.shape[:3] + (weight.shape[0],), jnp.float32)
    for tap_row in range(3):
        for tap_col in range(3):
            window = padded[:, 2 - tap_row:2 - tap_row + row_count, 2 - tap_col:2 - tap_col + col_count, :]
            total = total + jnp.einsum("bhxo,io->bhxi", window, weight_wide[:, tap_row, tap_col, :], precision=lax.Precision.HIGHEST)
    return total


def correlate(values, upstream):
    row_count = upstream.shape[1]
    col_count = upstream.shape[2]
    padded = jnp.pad(values.astype(jnp.float32), ((0, 0), (1, 1), (1, 1), (0, 0)))
    upstream_wide = upstream.astype(jnp.float32)
    terms = []
    for tap_row in range(3):
        for tap_col in range(3):
            window = padded[:, tap_row:tap_row + row_count, tap_col:tap_col + col_count, :]
            terms.append(jnp.einsum("bhxi,bhxo->io", window, upstream_wide, precision=lax.Precision.HIGHEST))
    stacked = jnp.stack(terms, axis=1)
    return stacked.reshape(values.shape[3], 3, 3, upstream.shape[3])


def reference(center_mid, radius_mid, conv_weight, center_upstream, radius_upstream):
    middle = center_mid.astype(jnp.float32)
    spread = radius_mid.astype(jnp.float32)
    act_upper = jnp.maximum(middle + spread, 0.0)
    act_lower = jnp.maximum(middle - spread, 0.0)
    center_hidden = ((act_upper + act_lower) * 0.5).astype(jnp.bfloat16)
    radius_hidden = ((act_upper - act_lower) * 0.5).astype(jnp.bfloat16)
    sign_weight = jnp.sign(conv_weight.astype(jnp.float32))
    weight_grad = (correlate(center_hidden, center_upstream) + sign_weight * correlate(radius_hidden, radius_upstream)) / BATCH
    center_hidden_cot = back_data(center_upstream, conv_weight).astype(jnp.bfloat16)
    radius_hidden_cot = back_data(radius_upstream, jnp.abs(conv_weight)).astype(jnp.bfloat16)
    upper_on = (center_mid > -radius_mid).astype(jnp.float32)
    lower_on = (center_mid > radius_mid).astype(jnp.float32)
    center_part = center_hidden_cot.astype(jnp.float32)
    radius_part = radius_hidden_cot.astype(jnp.float32)
    upper_cot = 0.5 * (center_part + radius_part) * upper_on
    lower_cot = 0.5 * (center_part - radius_part) * lower_on
    center_mid_grad = (upper_cot + lower_cot).astype(jnp.bfloat16)
    radius_mid_grad = (upper_cot - lower_cot).astype(jnp.bfloat16)
    return (center_mid_grad, radius_mid_grad, weight_grad)
```

```python
import jax
import jax.numpy as jnp
from jax import lax
from jax.experimental import pallas as pl
from jax.experimental.pallas import tpu as pltpu
from jax.sharding import PartitionSpec as P

MESH = pl.DeviceIdType.MESH
F32 = jnp.float32
BF16 = jnp.bfloat16


def place(x, y, z, c):
    return ((y * 2 + lax.rem(z, 2)) * 2 + c, (z // 2) * 4 + x)


def remote(src, dst, send, recv, where):
    return pltpu.make_async_remote_copy(
        src_ref=src, dst_ref=dst, send_sem=send, recv_sem=recv, device_id=where, device_id_type=MESH
    )


def mul(value, by):
    return pl.multiple_of(value, by)


def kernel(
    cm_hbm, rm_hbm, gc_hbm, gr_hbm, w_ref,
    cm_out, rm_out, wg_out,
    cm, rm, vsend, vbuf, vt, gbuf, wbuf, acc, rs_out, rs_in, b_out, b_in, halo_out, halo_in, total, r_out, r_in,
    load_sem, gload_sem, v_send, v_recv, vh_send, vh_recv, g_send, g_recv, p_send, p_recv,
    w_send, w_recv, wz_send, wz_recv, rs_send, rs_recv, b_send, b_recv, h_send, h_recv, r_send, r_recv,
):
    i_img, i_rows = lax.axis_index("img"), lax.axis_index("rows")
    x, z_hi = lax.rem(i_rows, 4), i_rows // 4
    y, z_lo, c = i_img // 4, lax.rem(i_img // 2, 2), lax.rem(i_img, 2)
    z = z_hi * 2 + z_lo
    block = x + 4 * c
    w_source = lax.rem(y, 4) == x
    w_core = y // 4
    part_core, part_half = z // 4, lax.rem(z // 2, 2)

    load_cm = pltpu.make_async_copy(cm_hbm, cm, load_sem.at[0])
    load_rm = pltpu.make_async_copy(rm_hbm, rm, load_sem.at[1])
    load_cm.start()
    load_rm.start()
    own_rows = pl.ds(mul(64 + 128 * x, 64), 128)

    def g_load(q, arr, ref):
        return pltpu.make_async_copy(
            ref.at[:, pl.ds(mul(128 * q, 128), 128)], gbuf.at[q, arr, c, own_rows], gload_sem.at[q, arr]
        )

    for q in range(4):
        g_load(q, 0, gc_hbm).start()
        g_load(q, 1, gr_hbm).start()

    barrier = pltpu.get_barrier_semaphore()

    def greet(where):
        pl.semaphore_signal(barrier, inc=1, device_id=where, device_id_type=MESH)

    def greet_ring(k, _):
        xd, cd = lax.rem(x + lax.rem(k, 4), 4), lax.rem(c + k // 4, 2)
        greet(place(xd, y, z, cd))
        return 0

    lax.fori_loop(1, 8, greet_ring, 0)

    def greet_z(k, _):
        greet(place(x, y, lax.rem(z + k, 8), c))
        return 0

    lax.fori_loop(1, 8, greet_z, 0)
    for cf in range(2):
        @pl.when(jnp.logical_or(y != block, c != cf))
        def _():
            greet(place(x, block, z, cf))

    b_self = jnp.logical_and(y == block, part_core == c)

    def greet_b(k, _):
        ys, half = k // 2, lax.rem(k, 2)
        xs, cs, zs = lax.rem(y, 4), y // 4, 2 * (2 * c + half) + z_lo
        same = (xs == x) & (ys == y) & (zs == z) & (cs == c)

        @pl.when(jnp.logical_not(same))
        def _():
            greet(place(xs, ys, zs, cs))
        return 0

    lax.fori_loop(0, 16, greet_b, 0)
    expected = (
        30
        + jnp.where(w_source, 8 - jnp.where(c == w_core, 1, 0), 0)
        - jnp.where(b_self, 1, 0)
    )

    zero_rows = jnp.zeros((64, 128), BF16)

    def clear(q, _):
        for arr in range(2):
            for image in range(2):
                gbuf[q, arr, image, 0:64, :] = zero_rows
                gbuf[q, arr, image, 576:640, :] = zero_rows
        return 0

    lax.fori_loop(0, 4, clear, 0)

    load_cm.wait()
    load_rm.wait()
    lane = lax.broadcasted_iota(jnp.int32, (128, 128), 1)
    for j in range(4):
        middle = cm[:, 128 * j : 128 * j + 128].astype(F32)
        spread = rm[:, 128 * j : 128 * j + 128].astype(F32)
        upper = jnp.maximum(middle + spread, 0.0)
        lower = jnp.maximum(middle - spread, 0.0)
        center = (upper + lower) * 0.5
        radius = (upper - lower) * 0.5
        vsend[2 * j] = jnp.where(lane < 64, center, pltpu.roll(radius, 64, 1)).astype(BF16)
        vsend[2 * j + 1] = jnp.where(lane < 64, pltpu.roll(center, 64, 1), radius).astype(BF16)

    pl.semaphore_wait(barrier, expected)

    def v_rows(xs):
        return pl.ds(mul(32 + 128 * xs, 32), 128)

    def v_copy(b):
        return remote(
            vsend.at[b], vbuf.at[c, v_rows(x)], v_send.at[b], v_recv.at[block],
            place(lax.rem(b, 4), y, z, b // 4),
        )

    def v_own():
        return pltpu.make_async_copy(vsend.at[block], vbuf.at[c, v_rows(x)], v_recv.at[block])

    v_own().start()

    def v_start(k, _):
        v_copy(lax.rem(block + k, 8)).start()
        return 0

    lax.fori_loop(1, 8, v_start, 0)

    def g_copy(q, xd):
        return remote(
            gbuf.at[q, :, c, own_rows], gbuf.at[q, :, c, own_rows], g_send.at[q, xd], g_recv.at[q, x],
            place(xd, y, z, c),
        )

    own_shard = z_lo * 2 + c

    def w_copy(q, yd):
        return remote(
            w_ref.at[q], wbuf.at[q, :, own_shard], w_send.at[q, yd], w_recv.at[q, c],
            place(x, yd, z, w_core),
        )

    def w_own(q):
        return pltpu.make_async_copy(w_ref.at[q], wbuf.at[q, :, own_shard], w_recv.at[q, c])

    def start_q(q, _):
        g_load(q, 0, gc_hbm).wait()
        g_load(q, 1, gr_hbm).wait()
        for k in range(1, 4):
            g_copy(q, lax.rem(x + k, 4)).start()

        @pl.when(w_source)
        def _():
            def to_y(k, _):
                w_copy(q, lax.rem(y + k, 8)).start()
                return 0

            lax.fori_loop(1, 8, to_y, 0)

            @pl.when(c == w_core)
            def _():
                w_own(q).start()

            @pl.when(c != w_core)
            def _():
                w_copy(q, y).start()
        return 0

    lax.fori_loop(0, 4, start_q, 0)

    for arr in range(2):
        acc[arr] = jnp.zeros((1152, 256), F32)

    def v_wait(b, _):
        pltpu.make_async_copy(vsend.at[b], vbuf.at[b // 4, v_rows(lax.rem(b, 4))], v_recv.at[b]).wait()
        return 0

    lax.fori_loop(0, 8, v_wait, 0)
    down, up = z_hi > 0, z_hi < 3
    z_down, z_up = lax.rem(z + 6, 8), lax.rem(z + 2, 8)
    vh_down = remote(
        vbuf.at[:, 32:64], vbuf.at[:, 544:576], vh_send.at[0], vh_recv.at[0], place(x, y, z_down, c)
    )
    vh_up = remote(
        vbuf.at[:, 512:544], vbuf.at[:, 0:32], vh_send.at[1], vh_recv.at[1], place(x, y, z_up, c)
    )

    @pl.when(down)
    def _():
        vh_down.start()

    @pl.when(up)
    def _():
        vh_up.start()

    def p_copy(q):
        ring_rows = gbuf.at[q, :, c, 64:576]
        return remote(ring_rows, ring_rows, p_send.at[q], p_recv.at[q], place(x, y, z, 1 - c))

    def p_wait(q):
        got = gbuf.at[q, :, 1 - c, 64:576]
        remote(got, got, p_send.at[q], p_recv.at[q], place(x, y, z, 1 - c)).wait_recv()

    ahead = lax.rem(z_lo + c, 2) == 0
    z_mate = lax.rem(jnp.where(ahead, z + 1, z + 7), 8)

    def wz_copy(q):
        half = wbuf.at[q, :, pl.ds(z_lo * 2, 2)]
        return remote(half, half, wz_send.at[q], wz_recv.at[q], place(x, y, z_mate, c))

    def wz_wait(q):
        half = wbuf.at[q, :, pl.ds((1 - z_lo) * 2, 2)]
        remote(half, half, wz_send.at[q], wz_recv.at[q], place(x, y, z_mate, c)).wait_recv()

    def forward(q):
        for k in range(1, 4):
            xs = lax.rem(x + k, 4)
            got = gbuf.at[q, :, c, pl.ds(mul(64 + 128 * xs, 64), 128)]
            remote(got, got, g_send.at[q, xs], g_recv.at[q, xs], place(xs, y, z, c)).wait_recv()
        p_copy(q).start()
        for cf in range(2):
            got = wbuf.at[q, :, z_lo * 2 + cf]
            pltpu.make_async_copy(w_ref.at[q], got, w_recv.at[q, cf]).wait()
        wz_copy(q).start()

    forward(0)

    @pl.when(down)
    def _():
        vh_up.wait_recv()

    @pl.when(up)
    def _():
        vh_down.wait_recv()

    @pl.when(jnp.logical_not(down))
    def _():
        vbuf[:, 0:32, :] = jnp.zeros((2, 32, 128), BF16)

    @pl.when(jnp.logical_not(up))
    def _():
        vbuf[:, 544:576, :] = jnp.zeros((2, 32, 128), BF16)

    column = lax.broadcasted_iota(jnp.int32, (64, 128), 0) & 31

    def turn(piece, _):
        vals = []
        for part in range(2):
            at = piece * 2 + part
            image, row = at // 9, lax.rem(at, 9)
            vals.append(vbuf[image, pl.ds(mul(row * 64, 64), 64), :].astype(F32))
        taps = [
            [jnp.where(column == 0, 0.0, pltpu.roll(v, 1, 0)) for v in vals],
            vals,
            [jnp.where(column == 31, 0.0, pltpu.roll(v, 63, 0)) for v in vals],
        ]
        for tap in range(3):
            turned = jnp.concatenate(taps[tap], axis=0).T.astype(BF16)
            for arr in range(2):
                vt[arr, tap * 64 : tap * 64 + 64, pl.ds(mul(piece * 128, 128), 128)] = turned[
                    arr * 64 : arr * 64 + 64
                ]
        return 0

    lax.fori_loop(0, 9, turn, 0)

    def rs_copy(q, zd):
        return remote(
            rs_out.at[q, zd], rs_in.at[q, z], rs_send.at[q, zd], rs_recv.at[q, z], place(x, y, zd, c)
        )

    def b_place(q, xf):
        return place(xf, block, 2 * q + z_lo, part_core)

    def b_is_self(q, xf):
        return (xf == x) & b_self & (q == z_hi)

    def b_copy(q, xf):
        return remote(
            b_out.at[q], b_in.at[y, part_half], b_send.at[q, xf], b_recv.at[y, part_half], b_place(q, xf)
        )

    def reduce_z(q):
        def one(zs, _):
            pltpu.make_async_copy(rs_out.at[q, zs], rs_in.at[q, zs], rs_recv.at[q, zs]).wait()
            return 0

        lax.fori_loop(0, 8, one, 0)
        value = rs_in[q, 0].astype(F32)
        for zs in range(1, 8):
            value = value + rs_in[q, zs].astype(F32)
        b_out[q] = value.astype(BF16)
        for k in range(4):
            xf = lax.rem(x + k, 4)

            @pl.when(b_is_self(q, xf))
            def _():
                pltpu.make_async_copy(
                    b_out.at[q], b_in.at[y, part_half], b_recv.at[y, part_half]
                ).start()

            @pl.when(jnp.logical_not(b_is_self(q, xf)))
            def _():
                b_copy(q, xf).start()

    def step(q, _):
        p_wait(q)
        wz_wait(q)
        kern = wbuf[q].reshape(192, 384)
        kern_abs = jnp.abs(kern)
        windows = []
        for arr in range(2):
            views = []
            for image in range(2):
                views.append(
                    jnp.concatenate(
                        [gbuf[q, arr, image, 64 - 32 * a : 640 - 32 * a, :] for a in range(3)], axis=1
                    )
                )
            windows.append(jnp.concatenate(views, axis=0))
        terms = [
            jnp.dot(vt[arr], windows[arr], preferred_element_type=F32) for arr in range(2)
        ]
        wide = kern.astype(F32)
        signed = jnp.where(wide > 0, terms[1], jnp.where(wide < 0, -terms[1], 0.0))
        partial = (terms[0] + signed).astype(BF16)
        for zd in range(8):
            shard, half = (zd % 2) * 2 + zd // 4, (zd // 2) % 2
            for k in range(5):
                a, tap = divmod(4 * half + k, 3)
                rs_out[q, zd, 16 * k : 16 * k + 16, :] = partial[
                    tap * 64 + shard * 16 : tap * 64 + shard * 16 + 16, a * 128 : a * 128 + 128
                ]
        pltpu.make_async_copy(rs_out.at[q, z], rs_in.at[q, z], rs_recv.at[q, z]).start()

        def rs_start(k, _):
            rs_copy(q, lax.rem(z + k, 8)).start()
            return 0

        lax.fori_loop(1, 8, rs_start, 0)
        for arr, factor in ((0, kern), (1, kern_abs)):
            acc[arr, :, 0:192] += lax.dot_general(
                windows[arr], factor, (((1,), (1,)), ((), ())), preferred_element_type=F32
            )

        @pl.when(q < 3)
        def _():
            forward(q + 1)

        @pl.when(q > 0)
        def _():
            reduce_z(q - 1)
        return 0

    lax.fori_loop(0, 4, step, 0)

    lane64 = lax.broadcasted_iota(jnp.int32, (64, 128), 1) < 64

    def fold(k, _):
        rows = pl.ds(mul(k * 64, 64), 64)
        c01, r01 = acc[0, rows, 0:128], acc[1, rows, 0:128]
        c2, r2 = acc[0, rows, 128:256], acc[1, rows, 128:256]
        first = jnp.where(lane64, c01, pltpu.roll(r01, 64, 1))
        middle = jnp.where(lane64, pltpu.roll(c01, 64, 1), r01)
        last = jnp.where(lane64, c2, pltpu.roll(r2, 64, 1))
        total[rows, :] = (
            middle
            + jnp.where(column == 31, 0.0, pltpu.roll(first, 63, 0))
            + jnp.where(column == 0, 0.0, pltpu.roll(last, 1, 0))
        )
        return 0

    lax.fori_loop(0, 18, fold, 0)
    for image in range(2):
        halo_out[0, image] = total[576 * image : 576 * image + 32, :]
        halo_out[1, image] = total[576 * image + 544 : 576 * image + 576, :]
    h_down = remote(halo_out.at[0], halo_in.at[0], h_send.at[0], h_recv.at[0], place(x, y, z_down, c))
    h_up = remote(halo_out.at[1], halo_in.at[1], h_send.at[1], h_recv.at[1], place(x, y, z_up, c))

    @pl.when(down)
    def _():
        h_down.start()

    @pl.when(up)
    def _():
        h_up.start()

    for image in range(2):
        r_out[image] = total[576 * image + 32 : 576 * image + 544, :].astype(BF16)

    def r_copy(b):
        return remote(
            r_out.at[b // 4, pl.ds(mul(128 * lax.rem(b, 4), 128), 128)], r_in.at[block],
            r_send.at[b], r_recv.at[block], place(lax.rem(b, 4), y, z, b // 4),
        )

    def r_send_to(b):
        @pl.when(b == block)
        def _():
            pltpu.make_async_copy(
                r_out.at[c, pl.ds(mul(128 * x, 128), 128)], r_in.at[block], r_recv.at[block]
            ).start()

        @pl.when(b != block)
        def _():
            r_copy(b).start()

    for b in (1, 2, 5, 6):
        r_send_to(b)
    reduce_z(3)

    @pl.when(up)
    def _():
        h_down.wait_recv()
        for image in range(2):
            r_out[image, 480:512, :] = (total[576 * image + 512 : 576 * image + 544, :] + halo_in[0, image]).astype(BF16)

    @pl.when(down)
    def _():
        h_up.wait_recv()
        for image in range(2):
            r_out[image, 0:32, :] = (total[576 * image + 32 : 576 * image + 64, :] + halo_in[1, image]).astype(BF16)

    for b in (0, 3, 4, 7):
        r_send_to(b)

    def r_wait(b, _):
        pltpu.make_async_copy(r_out.at[0, 0:128], r_in.at[b], r_recv.at[b]).wait()
        return 0

    lax.fori_loop(0, 8, r_wait, 0)
    low = lane < 64
    for j in range(4):
        lanes = slice(128 * j, 128 * j + 128)
        even, odd = r_in[2 * j].astype(F32), r_in[2 * j + 1].astype(F32)
        center = jnp.where(low, even, pltpu.roll(odd, 64, 1))
        radius = jnp.where(low, pltpu.roll(even, 64, 1), odd)
        middle, spread = cm[:, lanes].astype(F32), rm[:, lanes].astype(F32)
        upper = jnp.where(middle > -spread, 0.5 * (center + radius), 0.0)
        lower = jnp.where(middle > spread, 0.5 * (center - radius), 0.0)
        cm_out[:, lanes] = (upper + lower).astype(BF16)
        rm_out[:, lanes] = (upper - lower).astype(BF16)

    def b_wait(k, _):
        ys, half = k // 2, lax.rem(k, 2)
        pltpu.make_async_copy(b_out.at[0], b_in.at[ys, half], b_recv.at[ys, half]).wait()
        return 0

    lax.fori_loop(0, 16, b_wait, 0)
    for half in range(2):
        value = b_in[0, half].astype(F32)
        for ys in range(1, 8):
            value = value + b_in[ys, half].astype(F32)
        value = value * (1.0 / 32.0)
        if half == 0:
            wg_out[0:80, :] = value
        else:
            wg_out[80:144, :] = value[16:80]

    def v_done(k, _):
        v_copy(lax.rem(block + k, 8)).wait_send()
        r_copy(lax.rem(block + k, 8)).wait_send()
        return 0

    lax.fori_loop(1, 8, v_done, 0)

    @pl.when(down)
    def _():
        vh_down.wait_send()
        h_down.wait_send()

    @pl.when(up)
    def _():
        vh_up.wait_send()
        h_up.wait_send()

    def q_done(q, _):
        for k in range(1, 4):
            g_copy(q, lax.rem(x + k, 4)).wait_send()

        @pl.when(w_source)
        def _():
            def to_y(k, _):
                w_copy(q, lax.rem(y + k, 8)).wait_send()
                return 0

            lax.fori_loop(1, 8, to_y, 0)

            @pl.when(c != w_core)
            def _():
                w_copy(q, y).wait_send()

        p_copy(q).wait_send()
        wz_copy(q).wait_send()

        def rs_done(k, _):
            rs_copy(q, lax.rem(z + k, 8)).wait_send()
            return 0

        lax.fori_loop(1, 8, rs_done, 0)
        for k in range(4):
            xf = lax.rem(x + k, 4)

            @pl.when(jnp.logical_not(b_is_self(q, xf)))
            def _():
                b_copy(q, xf).wait_send()
        return 0

    lax.fori_loop(0, 4, q_done, 0)


def on_device(center_mid, radius_mid, conv_weight, center_upstream, radius_upstream):
    flat = [v.reshape(128, 512) for v in (center_mid, radius_mid, center_upstream, radius_upstream)]
    weight = conv_weight.reshape(16, 3, 3, 4, 128).transpose(3, 2, 0, 1, 4).reshape(4, 3, 16, 384)
    dma = pltpu.SemaphoreType.DMA
    hbm, vmem = pl.BlockSpec(memory_space=pl.ANY), pl.BlockSpec(memory_space=pltpu.VMEM)
    center_grad, radius_grad, weight_grad = pl.pallas_call(
        kernel,
        out_shape=(
            jax.ShapeDtypeStruct((128, 512), BF16),
            jax.ShapeDtypeStruct((128, 512), BF16),
            jax.ShapeDtypeStruct((144, 128), F32),
        ),
        in_specs=[hbm, hbm, hbm, hbm, vmem],
        out_specs=(vmem, vmem, vmem),
        scratch_shapes=[
            pltpu.VMEM((128, 512), BF16),
            pltpu.VMEM((128, 512), BF16),
            pltpu.VMEM((8, 128, 128), BF16),
            pltpu.VMEM((2, 576, 128), BF16),
            pltpu.VMEM((2, 192, 1152), BF16),
            pltpu.VMEM((4, 2, 2, 640, 128), BF16),
            pltpu.VMEM((4, 3, 4, 16, 384), BF16),
            pltpu.VMEM((2, 1152, 256), F32),
            pltpu.VMEM((4, 8, 80, 128), BF16),
            pltpu.VMEM((4, 8, 80, 128), BF16),
            pltpu.VMEM((4, 80, 128), BF16),
            pltpu.VMEM((8, 2, 80, 128), BF16),
            pltpu.VMEM((2, 2, 32, 128), F32),
            pltpu.VMEM((2, 2, 32, 128), F32),
            pltpu.VMEM((1152, 128), F32),
            pltpu.VMEM((2, 512, 128), BF16),
            pltpu.VMEM((8, 128, 128), BF16),
            dma((2,)), dma((4, 2)), dma((8,)), dma((8,)), dma((2,)), dma((2,)), dma((4, 4)), dma((4, 4)),
            dma((4,)), dma((4,)), dma((4, 8)), dma((4, 2)), dma((4,)), dma((4,)), dma((4, 8)), dma((4, 8)),
            dma((4, 4)), dma((8, 2)), dma((2,)), dma((2,)), dma((8,)), dma((8,)),
        ],
        compiler_params=pltpu.CompilerParams(
            collective_id=0, has_side_effects=True, vmem_limit_bytes=48 << 20
        ),
    )(flat[0], flat[1], flat[2], flat[3], weight)
    x = lax.rem(lax.axis_index("rows"), 4)
    own = lax.dynamic_slice_in_dim(weight_grad, x * 32, 32, axis=1)
    return (
        center_grad.reshape(center_mid.shape),
        radius_grad.reshape(center_mid.shape),
        own.reshape(3, 3, 16, 32).transpose(2, 0, 1, 3),
    )


def solution(mesh):
    placed = (
        P("img", "rows", None, None),
        P("img", "rows", None, None),
        P("img", None, None, None),
        P("img", "rows", None, None),
        P("img", "rows", None, None),
    )
    return jax.shard_map(
        on_device,
        mesh=mesh,
        in_specs=placed,
        out_specs=(
            P("img", "rows", None, None),
            P("img", "rows", None, None),
            P("img", None, None, "rows"),
        ),
        check_vma=False,
    )
```

```python
import jax
import jax.numpy as jnp
from jax import lax
from jax.experimental import pallas as pl
from jax.experimental.pallas import tpu as pltpu
from jax.sharding import PartitionSpec as P

MESH = pl.DeviceIdType.MESH
F32 = jnp.float32
BF16 = jnp.bfloat16


def place(x, y, z, c):
    return ((y * 2 + lax.rem(z, 2)) * 2 + c, (z // 2) * 4 + x)


def remote(src, dst, send, recv, where):
    return pltpu.make_async_remote_copy(
        src_ref=src, dst_ref=dst, send_sem=send, recv_sem=recv, device_id=where, device_id_type=MESH
    )


def mul(value, by):
    return pl.multiple_of(value, by)


def kernel(
    cm_hbm, rm_hbm, gc_hbm, gr_hbm, w_ref,
    cm_out, rm_out, wg_out,
    cm, rm, vsend, vbuf, vt, gbuf, wbuf, acc, rs_out, rs_in, a_out, a_in, c_out, c_in, halo_out, halo_in, total, r_out, r_in,
    load_sem, gload_sem, v_send, v_recv, vh_send, vh_recv, g_send, g_recv, p_send, p_recv,
    w_send, w_recv, wz_send, wz_recv, rs_send, rs_recv, a_send, a_recv, c_send, c_recv, h_send, h_recv, r_send, r_recv,
):
    i_img, i_rows = lax.axis_index("img"), lax.axis_index("rows")
    x, z_hi = lax.rem(i_rows, 4), i_rows // 4
    y, z_lo, c = i_img // 4, lax.rem(i_img // 2, 2), lax.rem(i_img, 2)
    z = z_hi * 2 + z_lo
    block = x + 4 * c
    w_source = lax.rem(y, 4) == x
    w_core = y // 4
    part_core, part_half = z // 4, lax.rem(z // 2, 2)

    load_cm = pltpu.make_async_copy(cm_hbm, cm, load_sem.at[0])
    load_rm = pltpu.make_async_copy(rm_hbm, rm, load_sem.at[1])
    load_cm.start()
    load_rm.start()
    own_rows = pl.ds(mul(64 + 128 * x, 64), 128)

    def g_load(q, arr, ref):
        return pltpu.make_async_copy(
            ref.at[:, pl.ds(mul(128 * q, 128), 128)], gbuf.at[q, arr, c, own_rows], gload_sem.at[q, arr]
        )

    for q in range(4):
        g_load(q, 0, gc_hbm).start()
        g_load(q, 1, gr_hbm).start()

    barrier = pltpu.get_barrier_semaphore()

    def greet(where):
        pl.semaphore_signal(barrier, inc=1, device_id=where, device_id_type=MESH)

    def greet_ring(k, _):
        xd, cd = lax.rem(x + lax.rem(k, 4), 4), lax.rem(c + k // 4, 2)
        greet(place(xd, y, z, cd))
        return 0

    lax.fori_loop(1, 8, greet_ring, 0)

    def greet_z(k, _):
        greet(place(x, y, lax.rem(z + k, 8), c))
        return 0

    lax.fori_loop(1, 8, greet_z, 0)
    def greet_y(k, _):
        greet(place(x, lax.rem(y + k, 8), z, c))
        return 0

    lax.fori_loop(1, 8, greet_y, 0)
    greet(place(x, block, z, 1 - c))
    q_own, u_own = y // 2, lax.rem(y, 2)
    own_part = (y == block) & (q_own == z_hi) & (part_core == c)

    def greet_owner(k, _):
        half, u = k // 2, lax.rem(k, 2)
        xs, ys, zs, cs = lax.rem(y, 4), 2 * z_hi + u, 2 * (2 * c + half) + z_lo, y // 4
        same = (xs == x) & (ys == y) & (zs == z) & (cs == c)

        @pl.when(jnp.logical_not(same))
        def _():
            greet(place(xs, ys, zs, cs))
        return 0

    lax.fori_loop(0, 4, greet_owner, 0)
    expected = (
        25 + jnp.where(w_source & (c != w_core), 8, 0) - jnp.where(own_part, 1, 0)
    )

    zero_rows = jnp.zeros((64, 128), BF16)

    def clear(q, _):
        for arr in range(2):
            for image in range(2):
                gbuf[q, arr, image, 0:64, :] = zero_rows
                gbuf[q, arr, image, 576:640, :] = zero_rows
        return 0

    lax.fori_loop(0, 4, clear, 0)

    load_cm.wait()
    load_rm.wait()
    lane = lax.broadcasted_iota(jnp.int32, (128, 128), 1)
    for j in range(4):
        middle = cm[:, 128 * j : 128 * j + 128].astype(F32)
        spread = rm[:, 128 * j : 128 * j + 128].astype(F32)
        upper = jnp.maximum(middle + spread, 0.0)
        lower = jnp.maximum(middle - spread, 0.0)
        center = (upper + lower) * 0.5
        radius = (upper - lower) * 0.5
        vsend[2 * j] = jnp.where(lane < 64, center, pltpu.roll(radius, 64, 1)).astype(BF16)
        vsend[2 * j + 1] = jnp.where(lane < 64, pltpu.roll(center, 64, 1), radius).astype(BF16)

    pl.semaphore_wait(barrier, expected)

    def v_rows(xs):
        return pl.ds(mul(32 + 128 * xs, 32), 128)

    def v_copy(b):
        return remote(
            vsend.at[b], vbuf.at[c, v_rows(x)], v_send.at[b], v_recv.at[block],
            place(lax.rem(b, 4), y, z, b // 4),
        )

    def v_own():
        return pltpu.make_async_copy(vsend.at[block], vbuf.at[c, v_rows(x)], v_recv.at[block])

    v_own().start()

    def v_start(k, _):
        v_copy(lax.rem(block + k, 8)).start()
        return 0

    lax.fori_loop(1, 8, v_start, 0)

    def g_copy(q, xd):
        return remote(
            gbuf.at[q, :, c, own_rows], gbuf.at[q, :, c, own_rows], g_send.at[q, xd], g_recv.at[q, x],
            place(xd, y, z, c),
        )

    own_shard = z_lo * 2 + c

    def w_copy(q, yd):
        return remote(
            w_ref.at[q], wbuf.at[q, :, own_shard], w_send.at[q, yd], w_recv.at[q, c],
            place(x, yd, z, w_core),
        )

    def w_own(q):
        return pltpu.make_async_copy(w_ref.at[q], wbuf.at[q, :, own_shard], w_recv.at[q, c])

    def start_q(q, _):
        g_load(q, 0, gc_hbm).wait()
        g_load(q, 1, gr_hbm).wait()
        for k in range(1, 4):
            g_copy(q, lax.rem(x + k, 4)).start()

        @pl.when(w_source)
        def _():
            def to_y(k, _):
                w_copy(q, lax.rem(y + k, 8)).start()
                return 0

            lax.fori_loop(1, 8, to_y, 0)

            @pl.when(c == w_core)
            def _():
                w_own(q).start()

            @pl.when(c != w_core)
            def _():
                w_copy(q, y).start()
        return 0

    lax.fori_loop(0, 4, start_q, 0)

    for arr in range(2):
        acc[arr] = jnp.zeros((1152, 256), F32)

    def v_wait(b, _):
        pltpu.make_async_copy(vsend.at[b], vbuf.at[b // 4, v_rows(lax.rem(b, 4))], v_recv.at[b]).wait()
        return 0

    lax.fori_loop(0, 8, v_wait, 0)
    down, up = z_hi > 0, z_hi < 3
    z_down, z_up = lax.rem(z + 6, 8), lax.rem(z + 2, 8)
    vh_down = remote(
        vbuf.at[:, 32:64], vbuf.at[:, 544:576], vh_send.at[0], vh_recv.at[0], place(x, y, z_down, c)
    )
    vh_up = remote(
        vbuf.at[:, 512:544], vbuf.at[:, 0:32], vh_send.at[1], vh_recv.at[1], place(x, y, z_up, c)
    )

    @pl.when(down)
    def _():
        vh_down.start()

    @pl.when(up)
    def _():
        vh_up.start()

    def p_copy(q):
        ring_rows = gbuf.at[q, :, c, 64:576]
        return remote(ring_rows, ring_rows, p_send.at[q], p_recv.at[q], place(x, y, z, 1 - c))

    def p_wait(q):
        got = gbuf.at[q, :, 1 - c, 64:576]
        remote(got, got, p_send.at[q], p_recv.at[q], place(x, y, z, 1 - c)).wait_recv()

    ahead = lax.rem(z_lo + c, 2) == 0
    z_mate = lax.rem(jnp.where(ahead, z + 1, z + 7), 8)

    def wz_copy(q):
        half = wbuf.at[q, :, pl.ds(z_lo * 2, 2)]
        return remote(half, half, wz_send.at[q], wz_recv.at[q], place(x, y, z_mate, c))

    def wz_wait(q):
        half = wbuf.at[q, :, pl.ds((1 - z_lo) * 2, 2)]
        remote(half, half, wz_send.at[q], wz_recv.at[q], place(x, y, z_mate, c)).wait_recv()

    def forward(q):
        for k in range(1, 4):
            xs = lax.rem(x + k, 4)
            got = gbuf.at[q, :, c, pl.ds(mul(64 + 128 * xs, 64), 128)]
            remote(got, got, g_send.at[q, xs], g_recv.at[q, xs], place(xs, y, z, c)).wait_recv()
        p_copy(q).start()
        for cf in range(2):
            got = wbuf.at[q, :, z_lo * 2 + cf]
            pltpu.make_async_copy(w_ref.at[q], got, w_recv.at[q, cf]).wait()
        wz_copy(q).start()

    forward(0)

    @pl.when(down)
    def _():
        vh_up.wait_recv()

    @pl.when(up)
    def _():
        vh_down.wait_recv()

    @pl.when(jnp.logical_not(down))
    def _():
        vbuf[:, 0:32, :] = jnp.zeros((2, 32, 128), BF16)

    @pl.when(jnp.logical_not(up))
    def _():
        vbuf[:, 544:576, :] = jnp.zeros((2, 32, 128), BF16)

    column = lax.broadcasted_iota(jnp.int32, (64, 128), 0) & 31

    def turn(piece, _):
        vals = []
        for part in range(2):
            at = piece * 2 + part
            image, row = at // 9, lax.rem(at, 9)
            vals.append(vbuf[image, pl.ds(mul(row * 64, 64), 64), :].astype(F32))
        taps = [
            [jnp.where(column == 0, 0.0, pltpu.roll(v, 1, 0)) for v in vals],
            vals,
            [jnp.where(column == 31, 0.0, pltpu.roll(v, 63, 0)) for v in vals],
        ]
        for tap in range(3):
            turned = jnp.concatenate(taps[tap], axis=0).T.astype(BF16)
            for arr in range(2):
                vt[arr, tap * 64 : tap * 64 + 64, pl.ds(mul(piece * 128, 128), 128)] = turned[
                    arr * 64 : arr * 64 + 64
                ]
        return 0

    lax.fori_loop(0, 9, turn, 0)

    def rs_copy(q, zd):
        return remote(
            rs_out.at[q, zd], rs_in.at[q, z], rs_send.at[q, zd], rs_recv.at[q, z], place(x, y, zd, c)
        )

    def a_copy(q, u):
        return remote(
            a_out.at[q, 32 * u : 32 * u + 48], a_in.at[y], a_send.at[q, u], a_recv.at[y],
            place(x, 2 * q + u, z, c),
        )

    def c_copy(xf):
        return remote(
            c_out, c_in.at[part_half, u_own], c_send.at[xf], c_recv.at[part_half, u_own],
            place(xf, block, 2 * q_own + z_lo, part_core),
        )

    def reduce_z(q):
        def one(zs, _):
            pltpu.make_async_copy(rs_out.at[q, zs], rs_in.at[q, zs], rs_recv.at[q, zs]).wait()
            return 0

        lax.fori_loop(0, 8, one, 0)
        value = rs_in[q, 0].astype(F32)
        for zs in range(1, 8):
            value = value + rs_in[q, zs].astype(F32)
        a_out[q] = value.astype(BF16)
        for u in range(2):
            @pl.when(y == 2 * q + u)
            def _():
                pltpu.make_async_copy(
                    a_out.at[q, 32 * u : 32 * u + 48], a_in.at[y], a_recv.at[y]
                ).start()

            @pl.when(y != 2 * q + u)
            def _():
                a_copy(q, u).start()

    def reduce_y():
        def one(ys, _):
            pltpu.make_async_copy(a_out.at[0, 0:48], a_in.at[ys], a_recv.at[ys]).wait()
            return 0

        lax.fori_loop(0, 8, one, 0)
        value = a_in[0].astype(F32)
        for ys in range(1, 8):
            value = value + a_in[ys].astype(F32)
        c_out[...] = value.astype(BF16)
        for k in range(4):
            xf = lax.rem(x + k, 4)
            if k == 0:
                @pl.when(own_part)
                def _():
                    pltpu.make_async_copy(
                        c_out, c_in.at[part_half, u_own], c_recv.at[part_half, u_own]
                    ).start()

                @pl.when(jnp.logical_not(own_part))
                def _():
                    c_copy(xf).start()
            else:
                c_copy(xf).start()

    def step(q, _):
        p_wait(q)
        wz_wait(q)
        kern = wbuf[q].reshape(192, 384)
        kern_abs = jnp.abs(kern)
        windows = []
        for arr in range(2):
            views = []
            for image in range(2):
                views.append(
                    jnp.concatenate(
                        [gbuf[q, arr, image, 64 - 32 * a : 640 - 32 * a, :] for a in range(3)], axis=1
                    )
                )
            windows.append(jnp.concatenate(views, axis=0))
        terms = [
            jnp.dot(vt[arr], windows[arr], preferred_element_type=F32) for arr in range(2)
        ]
        wide = kern.astype(F32)
        signed = jnp.where(wide > 0, terms[1], jnp.where(wide < 0, -terms[1], 0.0))
        partial = (terms[0] + signed).astype(BF16)
        for zd in range(8):
            shard, half = (zd % 2) * 2 + zd // 4, (zd // 2) % 2
            for k in range(5):
                a, tap = divmod(4 * half + k, 3)
                rs_out[q, zd, 16 * k : 16 * k + 16, :] = partial[
                    tap * 64 + shard * 16 : tap * 64 + shard * 16 + 16, a * 128 : a * 128 + 128
                ]
        pltpu.make_async_copy(rs_out.at[q, z], rs_in.at[q, z], rs_recv.at[q, z]).start()

        def rs_start(k, _):
            rs_copy(q, lax.rem(z + k, 8)).start()
            return 0

        lax.fori_loop(1, 8, rs_start, 0)
        for arr, factor in ((0, kern), (1, kern_abs)):
            acc[arr, :, 0:192] += lax.dot_general(
                windows[arr], factor, (((1,), (1,)), ((), ())), preferred_element_type=F32
            )

        @pl.when(q < 3)
        def _():
            forward(q + 1)

        @pl.when(q > 0)
        def _():
            reduce_z(q - 1)
        return 0

    lax.fori_loop(0, 4, step, 0)

    lane64 = lax.broadcasted_iota(jnp.int32, (64, 128), 1) < 64

    def fold(k, _):
        rows = pl.ds(mul(k * 64, 64), 64)
        c01, r01 = acc[0, rows, 0:128], acc[1, rows, 0:128]
        c2, r2 = acc[0, rows, 128:256], acc[1, rows, 128:256]
        first = jnp.where(lane64, c01, pltpu.roll(r01, 64, 1))
        middle = jnp.where(lane64, pltpu.roll(c01, 64, 1), r01)
        last = jnp.where(lane64, c2, pltpu.roll(r2, 64, 1))
        total[rows, :] = (
            middle
            + jnp.where(column == 31, 0.0, pltpu.roll(first, 63, 0))
            + jnp.where(column == 0, 0.0, pltpu.roll(last, 1, 0))
        )
        return 0

    lax.fori_loop(0, 18, fold, 0)
    for image in range(2):
        halo_out[0, image] = total[576 * image : 576 * image + 32, :]
        halo_out[1, image] = total[576 * image + 544 : 576 * image + 576, :]
    h_down = remote(halo_out.at[0], halo_in.at[0], h_send.at[0], h_recv.at[0], place(x, y, z_down, c))
    h_up = remote(halo_out.at[1], halo_in.at[1], h_send.at[1], h_recv.at[1], place(x, y, z_up, c))

    @pl.when(down)
    def _():
        h_down.start()

    @pl.when(up)
    def _():
        h_up.start()

    for image in range(2):
        r_out[image] = total[576 * image + 32 : 576 * image + 544, :].astype(BF16)

    def r_copy(b):
        return remote(
            r_out.at[b // 4, pl.ds(mul(128 * lax.rem(b, 4), 128), 128)], r_in.at[block],
            r_send.at[b], r_recv.at[block], place(lax.rem(b, 4), y, z, b // 4),
        )

    def r_send_to(b):
        @pl.when(b == block)
        def _():
            pltpu.make_async_copy(
                r_out.at[c, pl.ds(mul(128 * x, 128), 128)], r_in.at[block], r_recv.at[block]
            ).start()

        @pl.when(b != block)
        def _():
            r_copy(b).start()

    for b in (1, 2, 5, 6):
        r_send_to(b)
    reduce_z(3)

    @pl.when(up)
    def _():
        h_down.wait_recv()
        for image in range(2):
            r_out[image, 480:512, :] = (total[576 * image + 512 : 576 * image + 544, :] + halo_in[0, image]).astype(BF16)

    @pl.when(down)
    def _():
        h_up.wait_recv()
        for image in range(2):
            r_out[image, 0:32, :] = (total[576 * image + 32 : 576 * image + 64, :] + halo_in[1, image]).astype(BF16)

    for b in (0, 3, 4, 7):
        r_send_to(b)

    reduce_y()

    def r_wait(b, _):
        pltpu.make_async_copy(r_out.at[0, 0:128], r_in.at[b], r_recv.at[b]).wait()
        return 0

    lax.fori_loop(0, 8, r_wait, 0)
    low = lane < 64
    for j in range(4):
        lanes = slice(128 * j, 128 * j + 128)
        even, odd = r_in[2 * j].astype(F32), r_in[2 * j + 1].astype(F32)
        center = jnp.where(low, even, pltpu.roll(odd, 64, 1))
        radius = jnp.where(low, pltpu.roll(even, 64, 1), odd)
        middle, spread = cm[:, lanes].astype(F32), rm[:, lanes].astype(F32)
        upper = jnp.where(middle > -spread, 0.5 * (center + radius), 0.0)
        lower = jnp.where(middle > spread, 0.5 * (center - radius), 0.0)
        cm_out[:, lanes] = (upper + lower).astype(BF16)
        rm_out[:, lanes] = (upper - lower).astype(BF16)

    def c_wait(k, _):
        half, u = k // 2, lax.rem(k, 2)
        pltpu.make_async_copy(c_out, c_in.at[half, u], c_recv.at[half, u]).wait()
        return 0

    lax.fori_loop(0, 4, c_wait, 0)
    for half in range(2):
        for u in range(2):
            first = 0 if half == u == 0 else 1
            wg_out[64 * half + 32 * u + 16 * first : 64 * half + 32 * u + 48, :] = (
                c_in[half, u, 16 * first : 48, :].astype(F32) * (1.0 / 32.0)
            )

    def v_done(k, _):
        v_copy(lax.rem(block + k, 8)).wait_send()
        r_copy(lax.rem(block + k, 8)).wait_send()
        return 0

    lax.fori_loop(1, 8, v_done, 0)

    @pl.when(down)
    def _():
        vh_down.wait_send()
        h_down.wait_send()

    @pl.when(up)
    def _():
        vh_up.wait_send()
        h_up.wait_send()

    def q_done(q, _):
        for k in range(1, 4):
            g_copy(q, lax.rem(x + k, 4)).wait_send()

        @pl.when(w_source)
        def _():
            def to_y(k, _):
                w_copy(q, lax.rem(y + k, 8)).wait_send()
                return 0

            lax.fori_loop(1, 8, to_y, 0)

            @pl.when(c != w_core)
            def _():
                w_copy(q, y).wait_send()

        p_copy(q).wait_send()
        wz_copy(q).wait_send()

        def rs_done(k, _):
            rs_copy(q, lax.rem(z + k, 8)).wait_send()
            return 0

        lax.fori_loop(1, 8, rs_done, 0)
        for u in range(2):
            @pl.when(y != 2 * q + u)
            def _():
                a_copy(q, u).wait_send()
        return 0

    lax.fori_loop(0, 4, q_done, 0)
    for k in range(4):
        if k == 0:
            @pl.when(jnp.logical_not(own_part))
            def _():
                c_copy(x).wait_send()
        else:
            c_copy(lax.rem(x + k, 4)).wait_send()


def on_device(center_mid, radius_mid, conv_weight, center_upstream, radius_upstream):
    flat = [v.reshape(128, 512) for v in (center_mid, radius_mid, center_upstream, radius_upstream)]
    weight = conv_weight.reshape(16, 3, 3, 4, 128).transpose(3, 2, 0, 1, 4).reshape(4, 3, 16, 384)
    dma = pltpu.SemaphoreType.DMA
    hbm, vmem = pl.BlockSpec(memory_space=pl.ANY), pl.BlockSpec(memory_space=pltpu.VMEM)
    center_grad, radius_grad, weight_grad = pl.pallas_call(
        kernel,
        out_shape=(
            jax.ShapeDtypeStruct((128, 512), BF16),
            jax.ShapeDtypeStruct((128, 512), BF16),
            jax.ShapeDtypeStruct((144, 128), F32),
        ),
        in_specs=[hbm, hbm, hbm, hbm, vmem],
        out_specs=(vmem, vmem, vmem),
        scratch_shapes=[
            pltpu.VMEM((128, 512), BF16),
            pltpu.VMEM((128, 512), BF16),
            pltpu.VMEM((8, 128, 128), BF16),
            pltpu.VMEM((2, 576, 128), BF16),
            pltpu.VMEM((2, 192, 1152), BF16),
            pltpu.VMEM((4, 2, 2, 640, 128), BF16),
            pltpu.VMEM((4, 3, 4, 16, 384), BF16),
            pltpu.VMEM((2, 1152, 256), F32),
            pltpu.VMEM((4, 8, 80, 128), BF16),
            pltpu.VMEM((4, 8, 80, 128), BF16),
            pltpu.VMEM((4, 80, 128), BF16),
            pltpu.VMEM((8, 48, 128), BF16),
            pltpu.VMEM((48, 128), BF16),
            pltpu.VMEM((2, 2, 48, 128), BF16),
            pltpu.VMEM((2, 2, 32, 128), F32),
            pltpu.VMEM((2, 2, 32, 128), F32),
            pltpu.VMEM((1152, 128), F32),
            pltpu.VMEM((2, 512, 128), BF16),
            pltpu.VMEM((8, 128, 128), BF16),
            dma((2,)), dma((4, 2)), dma((8,)), dma((8,)), dma((2,)), dma((2,)), dma((4, 4)), dma((4, 4)),
            dma((4,)), dma((4,)), dma((4, 8)), dma((4, 2)), dma((4,)), dma((4,)), dma((4, 8)), dma((4, 8)),
            dma((4, 2)), dma((8,)), dma((4,)), dma((2, 2)), dma((2,)), dma((2,)), dma((8,)), dma((8,)),
        ],
        compiler_params=pltpu.CompilerParams(
            collective_id=0, has_side_effects=True, vmem_limit_bytes=48 << 20
        ),
    )(flat[0], flat[1], flat[2], flat[3], weight)
    x = lax.rem(lax.axis_index("rows"), 4)
    own = lax.dynamic_slice_in_dim(weight_grad, x * 32, 32, axis=1)
    return (
        center_grad.reshape(center_mid.shape),
        radius_grad.reshape(center_mid.shape),
        own.reshape(3, 3, 16, 32).transpose(2, 0, 1, 3),
    )


def solution(mesh):
    placed = (
        P("img", "rows", None, None),
        P("img", "rows", None, None),
        P("img", None, None, None),
        P("img", "rows", None, None),
        P("img", "rows", None, None),
    )
    return jax.shard_map(
        on_device,
        mesh=mesh,
        in_specs=placed,
        out_specs=(
            P("img", "rows", None, None),
            P("img", "rows", None, None),
            P("img", None, None, "rows"),
        ),
        check_vma=False,
    )
```

```python
import jax
import jax.numpy as jnp
from jax import lax
from jax.experimental import pallas as pl
from jax.experimental.pallas import tpu as pltpu
from jax.sharding import PartitionSpec as P

MESH = pl.DeviceIdType.MESH
F32 = jnp.float32
BF16 = jnp.bfloat16
NQ = 4
LANES = 512 // NQ
QB = 4 // NQ


def rem(value, by):
    return lax.rem(value, jnp.int32(by))


def div(value, by):
    return lax.div(value, jnp.int32(by))


def place(x, y, z, c):
    return ((y * 2 + rem(z, 2)) * 2 + c, div(z, 2) * 4 + x)


def remote(src, dst, send, recv, where):
    return pltpu.make_async_remote_copy(
        src_ref=src, dst_ref=dst, send_sem=send, recv_sem=recv, device_id=where, device_id_type=MESH
    )


def local(src, dst, sem):
    return pltpu.make_async_copy(src, dst, sem)


def bytes_of(ref, sem):
    pltpu.make_async_copy(ref, ref, sem).wait()


def mul(value, by):
    return pl.multiple_of(value, by)


def kernel(
    cm_hbm, rm_hbm, gc_hbm, gr_hbm, w_ref,
    cm_out, rm_out, wg_out,
    cm, rm, vsend, vmain, vhalo, vt, gbuf, wbuf, acc, rs_out, rs_in, a_out, a_in, c_out, c_in,
    halo_out, halo_in, total, r_out, r_in,
    load_sem, gload_sem, v_send, v_recv, vh_send, vh_recv, g_send, g_recv, p_send, p_recv,
    w_send, w_recv, wz_send, wz_recv, rs_send, rs_recv, a_send, a_recv, c_send, c_recv,
    h_send, h_recv, r_send, r_recv,
):
    i_img, i_rows = lax.axis_index("img"), lax.axis_index("rows")
    x, z_hi = rem(i_rows, 4), div(i_rows, 4)
    y, z_lo, c = div(i_img, 4), rem(div(i_img, 2), 2), rem(i_img, 2)
    z = z_hi * 2 + z_lo
    block = x + 4 * c
    w_source = rem(y, 4) == x
    w_core = div(y, 4)
    part_core, part_half = div(z, 4), rem(div(z, 2), 2)
    q_own, u_own = div(y, 2), rem(y, 2)
    own_part = (y == block) & (q_own == z_hi) & (part_core == c)

    barrier = pltpu.get_barrier_semaphore()

    def greet(where):
        pl.semaphore_signal(barrier, inc=1, device_id=where, device_id_type=MESH)

    for k in range(1, 8):
        greet(place(rem(x + k, 4), y, z, rem(c + k // 4, 2)))
        greet(place(x, y, rem(z + k, 8), c))
        greet(place(x, rem(y + k, 8), z, c))
    greet(place(x, block, z, 1 - c))
    for half in range(2):
        for u in range(2):
            xs, ys, zs, cs = rem(y, 4), 2 * z_hi + u, 2 * (2 * c + half) + z_lo, div(y, 4)
            same = (xs == x) & (ys == y) & (zs == z) & (cs == c)

            @pl.when(jnp.logical_not(same))
            def _():
                greet(place(xs, ys, zs, cs))

    expected = 25 + jnp.where(w_source & (c != w_core), 8, 0) - jnp.where(own_part, 1, 0)

    load_cm = local(cm_hbm, cm, load_sem.at[0])
    load_rm = local(rm_hbm, rm, load_sem.at[1])
    load_cm.start()
    load_rm.start()
    own_rows = pl.ds(mul(64 + 128 * x, 64), 128)
    for q in range(NQ):
        for arr, ref in ((0, gc_hbm), (1, gr_hbm)):
            local(
                ref.at[:, LANES * q : LANES * q + LANES], gbuf.at[q, arr, c, own_rows], gload_sem.at[q]
            ).start()

    load_cm.wait()
    load_rm.wait()
    lane = lax.broadcasted_iota(jnp.int32, (128, 128), 1)
    low = lane < 64
    for j in range(4):
        middle = cm[:, 128 * j : 128 * j + 128].astype(F32)
        spread = rm[:, 128 * j : 128 * j + 128].astype(F32)
        upper = jnp.maximum(middle + spread, 0.0)
        lower = jnp.maximum(middle - spread, 0.0)
        center = (upper + lower) * 0.5
        radius = (upper - lower) * 0.5
        vsend[2 * j] = jnp.where(low, center, pltpu.roll(radius, 64, 1)).astype(BF16)
        vsend[2 * j + 1] = jnp.where(low, pltpu.roll(center, 64, 1), radius).astype(BF16)

    pl.semaphore_wait(barrier, expected)

    v_place = vmain.at[c, pl.ds(mul(128 * x, 128), 128)]
    for k in range(1, 8):
        xd, cd = rem(x + k, 4), rem(c + k // 4, 2)
        remote(vsend.at[xd + 4 * cd], v_place, v_send, v_recv, place(xd, y, z, cd)).start()
    local(vsend.at[block], v_place, v_recv).start()

    own_shard = z_lo * 2 + c

    def start_w(q):
        @pl.when(w_source)
        def _():
            for k in range(1, 8):
                remote(
                    w_ref.at[q], wbuf.at[q, :, own_shard], w_send, w_recv.at[q],
                    place(x, rem(y + k, 8), z, w_core),
                ).start()

            @pl.when(c == w_core)
            def _():
                local(w_ref.at[q], wbuf.at[q, :, own_shard], w_recv.at[q]).start()

            @pl.when(c != w_core)
            def _():
                remote(
                    w_ref.at[q], wbuf.at[q, :, own_shard], w_send, w_recv.at[q], place(x, y, z, w_core)
                ).start()

    def start_g(q):
        own = gbuf.at[q, :, c, own_rows]
        bytes_of(own, gload_sem.at[q])
        for k in range(1, 4):
            remote(own, own, g_send, g_recv.at[q], place(rem(x + k, 4), y, z, c)).start()

    for q in range(NQ):
        start_w(q)
        start_g(q)

    zero_rows = jnp.zeros((64, LANES), BF16)

    def clear(q, _):
        for arr in range(2):
            for image in range(2):
                gbuf[q, arr, image, 0:64, :] = zero_rows
                gbuf[q, arr, image, 576:640, :] = zero_rows
        return 0

    lax.fori_loop(0, NQ, clear, 0)
    for arr in range(2):
        acc[arr] = jnp.zeros((1152, 256), F32)

    bytes_of(vmain, v_recv)
    down, up = z_hi > 0, z_hi < 3
    at_down, at_up = place(x, y, rem(z + 6, 8), c), place(x, y, rem(z + 2, 8), c)
    vh_down = remote(vmain.at[:, 0:32], vhalo.at[:, 1], vh_send.at[0], vh_recv.at[0], at_down)
    vh_up = remote(vmain.at[:, 480:512], vhalo.at[:, 0], vh_send.at[1], vh_recv.at[1], at_up)

    @pl.when(down)
    def _():
        vh_down.start()

    @pl.when(up)
    def _():
        vh_up.start()

    column = lax.broadcasted_iota(jnp.int32, (128, 128), 0) & 31

    def turn(v, piece):
        taps = (
            jnp.where(column == 0, 0.0, pltpu.roll(v, 1, 0)),
            v,
            jnp.where(column == 31, 0.0, pltpu.roll(v, 127, 0)),
        )
        for tap in range(3):
            turned = taps[tap].T.astype(BF16)
            for arr in range(2):
                vt[arr, tap * 64 : tap * 64 + 64, 128 * piece : 128 * piece + 128] = turned[
                    arr * 64 : arr * 64 + 64
                ]

    for piece in range(8):
        turn(vmain[piece // 4, 128 * (piece % 4) : 128 * (piece % 4) + 128, :].astype(F32), piece)

    ahead = rem(z_lo + c, 2) == 0
    at_mate = place(x, y, rem(jnp.where(ahead, z + 1, z + 7), 8), c)
    at_twin = place(x, y, z, 1 - c)

    def forward(q):
        bytes_of(gbuf.at[q, :, c, 64:448], g_recv.at[q])
        ring_rows = gbuf.at[q, :, c, 64:576]
        remote(ring_rows, ring_rows, p_send, p_recv.at[q], at_twin).start()
        shards = wbuf.at[q, :, pl.ds(z_lo * 2, 2)]
        bytes_of(shards, w_recv.at[q])
        remote(shards, shards, wz_send, wz_recv.at[q], at_mate).start()

    forward(0)

    @pl.when(down)
    def _():
        vh_up.wait_recv()

    @pl.when(up)
    def _():
        vh_down.wait_recv()

    @pl.when(jnp.logical_not(down))
    def _():
        vhalo[:, 0] = jnp.zeros((2, 32, 128), BF16)

    @pl.when(jnp.logical_not(up))
    def _():
        vhalo[:, 1] = jnp.zeros((2, 32, 128), BF16)

    turn(vhalo[...].astype(F32).reshape(128, 128), 8)

    def reduce_z(q):
        bytes_of(rs_in.at[q], rs_recv.at[q])
        for qb in range(QB):
            rows = slice(80 * qb, 80 * qb + 80)
            value = rs_in[q, 0, rows].astype(F32)
            for zs in range(1, 8):
                value = value + rs_in[q, zs, rows].astype(F32)
            a_out[q, qb] = value.astype(BF16)
            for u in range(2):
                piece = a_out.at[q, qb, 32 * u : 32 * u + 48]
                to = 2 * (q * QB + qb) + u

                @pl.when(y == to)
                def _():
                    local(piece, a_in.at[y], a_recv).start()

                @pl.when(y != to)
                def _():
                    remote(piece, a_in.at[y], a_send, a_recv, place(x, to, z, c)).start()

    def step(q, _):
        @pl.when(q < NQ - 1)
        def _():
            forward(q + 1)

        bytes_of(gbuf.at[q, :, 1 - c, 64:576], p_recv.at[q])
        bytes_of(wbuf.at[q, :, pl.ds((1 - z_lo) * 2, 2)], wz_recv.at[q])
        kern = wbuf[q].reshape(192, 3 * LANES)
        windows = []
        for arr in range(2):
            views = []
            for image in range(2):
                views.append(
                    jnp.concatenate(
                        [gbuf[q, arr, image, 96 - 32 * a : 608 - 32 * a, :] for a in range(3)], axis=1
                    )
                )
            for image in range(2):
                for first in (64, 608):
                    views.append(
                        jnp.concatenate(
                            [gbuf[q, arr, image, first - 32 * a : first + 32 - 32 * a, :] for a in range(3)],
                            axis=1,
                        )
                    )
            windows.append(jnp.concatenate(views, axis=0))
        terms = [jnp.dot(vt[arr], windows[arr], preferred_element_type=F32) for arr in range(2)]
        wide = kern.astype(F32)
        signed = jnp.where(wide > 0, terms[1], jnp.where(wide < 0, -terms[1], 0.0))
        partial = (terms[0] + signed).astype(BF16)
        for zd in range(8):
            shard, half = (zd % 2) * 2 + zd // 4, (zd // 2) % 2
            for qb in range(QB):
                for k in range(5):
                    a, tap = divmod(4 * half + k, 3)
                    rs_out[q, zd, 80 * qb + 16 * k : 80 * qb + 16 * k + 16, :] = partial[
                        tap * 64 + shard * 16 : tap * 64 + shard * 16 + 16,
                        a * LANES + 128 * qb : a * LANES + 128 * qb + 128,
                    ]
        local(rs_out.at[q, z], rs_in.at[q, z], rs_recv.at[q]).start()
        for k in range(1, 8):
            zd = rem(z + k, 8)
            remote(rs_out.at[q, zd], rs_in.at[q, z], rs_send, rs_recv.at[q], place(x, y, zd, c)).start()
        for arr, factor in ((0, kern), (1, jnp.abs(kern))):
            acc[arr, :, 0:192] += lax.dot_general(
                windows[arr], factor, (((1,), (1,)), ((), ())), preferred_element_type=F32
            )

        @pl.when(q > 0)
        def _():
            reduce_z(q - 1)
        return 0

    lax.fori_loop(0, NQ, step, 0)

    column64 = lax.broadcasted_iota(jnp.int32, (64, 128), 0) & 31
    low64 = lax.broadcasted_iota(jnp.int32, (64, 128), 1) < 64

    def fold(k, _):
        rows = pl.ds(mul(k * 64, 64), 64)
        c01, r01 = acc[0, rows, 0:128], acc[1, rows, 0:128]
        c2, r2 = acc[0, rows, 128:256], acc[1, rows, 128:256]
        first = jnp.where(low64, c01, pltpu.roll(r01, 64, 1))
        middle = jnp.where(low64, pltpu.roll(c01, 64, 1), r01)
        last = jnp.where(low64, c2, pltpu.roll(r2, 64, 1))
        value = (
            middle
            + jnp.where(column64 == 31, 0.0, pltpu.roll(first, 63, 0))
            + jnp.where(column64 == 0, 0.0, pltpu.roll(last, 1, 0))
        )
        total[rows, :] = value
        return 0

    lax.fori_loop(16, 18, fold, 0)
    for image in range(2):
        for side in range(2):
            first = 1024 + 64 * image + 32 * side
            halo_out[side, image] = total[first : first + 32, :]
    h_down = remote(halo_out.at[0], halo_in.at[0], h_send.at[0], h_recv.at[0], at_down)
    h_up = remote(halo_out.at[1], halo_in.at[1], h_send.at[1], h_recv.at[1], at_up)

    @pl.when(down)
    def _():
        h_down.start()

    @pl.when(up)
    def _():
        h_up.start()

    lax.fori_loop(0, 16, fold, 0)
    for image in range(2):
        r_out[image] = total[512 * image : 512 * image + 512, :].astype(BF16)

    def r_start(b):
        @pl.when(b == block)
        def _():
            local(r_out.at[c, pl.ds(mul(128 * x, 128), 128)], r_in.at[block], r_recv).start()

        @pl.when(b != block)
        def _():
            remote(
                r_out.at[b // 4, 128 * (b % 4) : 128 * (b % 4) + 128], r_in.at[block], r_send, r_recv,
                place(b % 4, y, z, b // 4),
            ).start()

    for b in (1, 2, 5, 6):
        r_start(b)
    reduce_z(NQ - 1)

    @pl.when(up)
    def _():
        h_down.wait_recv()
        for image in range(2):
            r_out[image, 480:512, :] = (total[512 * image + 480 : 512 * image + 512, :] + halo_in[0, image]).astype(BF16)

    @pl.when(down)
    def _():
        h_up.wait_recv()
        for image in range(2):
            r_out[image, 0:32, :] = (total[512 * image : 512 * image + 32, :] + halo_in[1, image]).astype(BF16)

    for b in (0, 3, 4, 7):
        r_start(b)

    bytes_of(a_in, a_recv)
    value = a_in[0].astype(F32)
    for ys in range(1, 8):
        value = value + a_in[ys].astype(F32)
    c_out[...] = value.astype(BF16)
    slot = c_in.at[2 * part_half + u_own]

    @pl.when(own_part)
    def _():
        local(c_out, slot, c_recv).start()

    @pl.when(jnp.logical_not(own_part))
    def _():
        remote(c_out, slot, c_send, c_recv, place(x, block, 2 * q_own + z_lo, part_core)).start()

    for k in range(1, 4):
        remote(
            c_out, slot, c_send, c_recv, place(rem(x + k, 4), block, 2 * q_own + z_lo, part_core)
        ).start()

    bytes_of(r_in, r_recv)
    for j in range(4):
        lanes = slice(128 * j, 128 * j + 128)
        even, odd = r_in[2 * j].astype(F32), r_in[2 * j + 1].astype(F32)
        center = jnp.where(low, even, pltpu.roll(odd, 64, 1))
        radius = jnp.where(low, pltpu.roll(even, 64, 1), odd)
        middle, spread = cm[:, lanes].astype(F32), rm[:, lanes].astype(F32)
        upper = jnp.where(middle > -spread, 0.5 * (center + radius), 0.0)
        lower = jnp.where(middle > spread, 0.5 * (center - radius), 0.0)
        cm_out[:, lanes] = (upper + lower).astype(BF16)
        rm_out[:, lanes] = (upper - lower).astype(BF16)

    bytes_of(vsend.at[0:7], v_send)
    bytes_of(r_in.at[0:7], r_send)

    @pl.when(down)
    def _():
        vh_down.wait_send()
        h_down.wait_send()

    @pl.when(up)
    def _():
        vh_up.wait_send()
        h_up.wait_send()

    bytes_of(gbuf.at[:, :, c, 64:448], g_send)
    bytes_of(gbuf.at[:, :, c, 64:576], p_send)
    bytes_of(wbuf.at[:, :, pl.ds(z_lo * 2, 2)], wz_send)

    @pl.when(w_source & (c == w_core))
    def _():
        bytes_of(acc.at[0, 0:1008], w_send)

    @pl.when(w_source & (c != w_core))
    def _():
        bytes_of(acc.at[0], w_send)

    bytes_of(rs_out.at[:, 0:7], rs_send)
    bytes_of(a_in.at[0:7], a_send)

    @pl.when(own_part)
    def _():
        bytes_of(c_in.at[0:3], c_send)

    @pl.when(jnp.logical_not(own_part))
    def _():
        bytes_of(c_in, c_send)

    bytes_of(c_in, c_recv)
    for half in range(2):
        for u in range(2):
            first = 0 if half == u == 0 else 1
            wg_out[64 * half + 32 * u + 16 * first : 64 * half + 32 * u + 48, :] = (
                c_in[2 * half + u, 16 * first : 48, :].astype(F32) * (1.0 / 32.0)
            )


def on_device(center_mid, radius_mid, conv_weight, center_upstream, radius_upstream):
    flat = [v.reshape(128, 512) for v in (center_mid, radius_mid, center_upstream, radius_upstream)]
    weight = conv_weight.reshape(16, 3, 3, NQ, LANES).transpose(3, 2, 0, 1, 4)
    weight = weight.reshape(NQ, 3, 16, 3 * LANES)
    dma = pltpu.SemaphoreType.DMA
    hbm, vmem = pl.BlockSpec(memory_space=pl.ANY), pl.BlockSpec(memory_space=pltpu.VMEM)
    center_grad, radius_grad, weight_grad = pl.pallas_call(
        kernel,
        out_shape=(
            jax.ShapeDtypeStruct((128, 512), BF16),
            jax.ShapeDtypeStruct((128, 512), BF16),
            jax.ShapeDtypeStruct((144, 128), F32),
        ),
        in_specs=[hbm, hbm, hbm, hbm, vmem],
        out_specs=(vmem, vmem, vmem),
        scratch_shapes=[
            pltpu.VMEM((128, 512), BF16),
            pltpu.VMEM((128, 512), BF16),
            pltpu.VMEM((8, 128, 128), BF16),
            pltpu.VMEM((2, 512, 128), BF16),
            pltpu.VMEM((2, 2, 32, 128), BF16),
            pltpu.VMEM((2, 192, 1152), BF16),
            pltpu.VMEM((NQ, 2, 2, 640, LANES), BF16),
            pltpu.VMEM((NQ, 3, 4, 16, 3 * LANES), BF16),
            pltpu.VMEM((2, 1152, 256), F32),
            pltpu.VMEM((NQ, 8, 80 * QB, 128), BF16),
            pltpu.VMEM((NQ, 8, 80 * QB, 128), BF16),
            pltpu.VMEM((NQ, QB, 80, 128), BF16),
            pltpu.VMEM((8, 48, 128), BF16),
            pltpu.VMEM((48, 128), BF16),
            pltpu.VMEM((4, 48, 128), BF16),
            pltpu.VMEM((2, 2, 32, 128), F32),
            pltpu.VMEM((2, 2, 32, 128), F32),
            pltpu.VMEM((1152, 128), F32),
            pltpu.VMEM((2, 512, 128), BF16),
            pltpu.VMEM((8, 128, 128), BF16),
            dma((2,)), dma((NQ,)), dma, dma, dma((2,)), dma((2,)), dma, dma((NQ,)), dma, dma((NQ,)),
            dma, dma((NQ,)), dma, dma((NQ,)), dma, dma((NQ,)), dma, dma, dma, dma,
            dma((2,)), dma((2,)), dma, dma,
        ],
        compiler_params=pltpu.CompilerParams(
            collective_id=0, has_side_effects=True, vmem_limit_bytes=48 << 20
        ),
    )(flat[0], flat[1], flat[2], flat[3], weight)
    x = lax.rem(lax.axis_index("rows"), 4)
    own = lax.dynamic_slice_in_dim(weight_grad, x * 32, 32, axis=1)
    return (
        center_grad.reshape(center_mid.shape),
        radius_grad.reshape(center_mid.shape),
        own.reshape(3, 3, 16, 32).transpose(2, 0, 1, 3),
    )


def solution(mesh):
    placed = (
        P("img", "rows", None, None),
        P("img", "rows", None, None),
        P("img", None, None, None),
        P("img", "rows", None, None),
        P("img", "rows", None, None),
    )
    return jax.shard_map(
        on_device,
        mesh=mesh,
        in_specs=placed,
        out_specs=(
            P("img", "rows", None, None),
            P("img", "rows", None, None),
            P("img", None, None, "rows"),
        ),
        check_vma=False,
    )
```

```python
import jax
import jax.numpy as jnp
from jax import lax
from jax.experimental import pallas as pl
from jax.experimental.pallas import tpu as pltpu
from jax.sharding import PartitionSpec as P

MESH = pl.DeviceIdType.MESH
F32 = jnp.float32
BF16 = jnp.bfloat16
NQ = 4
LANES = 512 // NQ
QB = 4 // NQ


def rem(value, by):
    return lax.rem(value, jnp.int32(by))


def div(value, by):
    return lax.div(value, jnp.int32(by))


def place(x, y, z, c):
    return ((y * 2 + rem(z, 2)) * 2 + c, div(z, 2) * 4 + x)


def remote(src, dst, send, recv, where):
    return pltpu.make_async_remote_copy(
        src_ref=src, dst_ref=dst, send_sem=send, recv_sem=recv, device_id=where, device_id_type=MESH
    )


def local(src, dst, sem):
    return pltpu.make_async_copy(src, dst, sem)


def bytes_of(ref, sem):
    pltpu.make_async_copy(ref, ref, sem).wait()


def mul(value, by):
    return pl.multiple_of(value, by)


def kernel(
    cm_hbm, rm_hbm, gc_hbm, gr_hbm, w_ref,
    cm_out, rm_out, wg_out,
    cm, rm, vsend, vmain, vhalo, vt, gbuf, wbuf, acc, rs_out, rs_in, ry_out, ry_in, a_out, a_in, ay_out, ay_in, c_out, c_in, cy_out, cy_in,
    halo_out, halo_in, total, r_out, r_in,
    load_sem, gload_sem, v_send, v_recv, vh_send, vh_recv, g_send, g_recv, p_send, p_recv,
    w_send, w_recv, wz_send, wz_recv, rs_send, rs_recv, ry_send, ry_recv, a_send, a_recv, ay_send, ay_recv, c_send, c_recv, cy_send, cy_recv,
    h_send, h_recv, r_send, r_recv,
):
    i_img, i_rows = lax.axis_index("img"), lax.axis_index("rows")
    x, z_hi = rem(i_rows, 4), div(i_rows, 4)
    y, z_lo, c = div(i_img, 4), rem(div(i_img, 2), 2), rem(i_img, 2)
    z = z_hi * 2 + z_lo
    block = x + 4 * c
    w_source = rem(y, 4) == x
    w_core = div(y, 4)
    part_core, part_half = div(z, 4), rem(div(z, 2), 2)
    sums_y = y == block
    part_own = part_core == c
    sums_z = z_lo == div(y, 4)
    core_y, half_y = rem(div(y, 2), 2), rem(y, 2)
    own_y = (y == block) & (core_y == c)

    barrier = pltpu.get_barrier_semaphore()

    def greet(where):
        pl.semaphore_signal(barrier, inc=1, device_id=where, device_id_type=MESH)

    for k in range(1, 8):
        greet(place(rem(x + k, 4), y, z, rem(c + k // 4, 2)))
        greet(place(x, y, rem(z + k, 8), c))
        greet(place(x, rem(y + k, 8), z, c))
    greet(place(x, block, z, 1 - c))
    for half in range(2):
        xs, zs, cs = rem(y, 4), 2 * (2 * c + half) + z_lo, div(y, 4)
        same = (xs == x) & (zs == z) & (cs == c)

        @pl.when(jnp.logical_not(same))
        def _():
            greet(place(xs, y, zs, cs))

        ys = 4 * z_lo + 2 * c + half
        same_y = (xs == x) & (ys == y) & (cs == c)

        @pl.when(jnp.logical_not(same_y))
        def _():
            greet(place(xs, ys, z, cs))

    expected = (
        21
        + jnp.where(sums_z, 4 - jnp.where(own_y, 1, 0), 0)
        + jnp.where(w_source & (c != w_core), 8, 0)
        + jnp.where(sums_y, 16 - jnp.where(part_own, 1, 0), 0)
    )

    load_cm = local(cm_hbm, cm, load_sem.at[0])
    load_rm = local(rm_hbm, rm, load_sem.at[1])
    load_cm.start()
    load_rm.start()
    own_rows = pl.ds(mul(64 + 128 * x, 64), 128)
    for q in range(NQ):
        for arr, ref in ((0, gc_hbm), (1, gr_hbm)):
            local(
                ref.at[:, LANES * q : LANES * q + LANES], gbuf.at[q, arr, c, own_rows], gload_sem.at[q]
            ).start()

    load_cm.wait()
    load_rm.wait()
    lane = lax.broadcasted_iota(jnp.int32, (128, 128), 1)
    low = lane < 64
    for j in range(4):
        middle = cm[:, 128 * j : 128 * j + 128].astype(F32)
        spread = rm[:, 128 * j : 128 * j + 128].astype(F32)
        upper = jnp.maximum(middle + spread, 0.0)
        lower = jnp.maximum(middle - spread, 0.0)
        center = (upper + lower) * 0.5
        radius = (upper - lower) * 0.5
        vsend[2 * j] = jnp.where(low, center, pltpu.roll(radius, 64, 1)).astype(BF16)
        vsend[2 * j + 1] = jnp.where(low, pltpu.roll(center, 64, 1), radius).astype(BF16)

    pl.semaphore_wait(barrier, expected)

    v_place = vmain.at[c, pl.ds(mul(128 * x, 128), 128)]
    for k in range(1, 8):
        xd, cd = rem(x + k, 4), rem(c + k // 4, 2)
        remote(vsend.at[xd + 4 * cd], v_place, v_send, v_recv, place(xd, y, z, cd)).start()
    local(vsend.at[block], v_place, v_recv).start()

    own_shard = z_lo * 2 + c

    def start_w(q):
        @pl.when(w_source)
        def _():
            for k in range(1, 8):
                remote(
                    w_ref.at[q], wbuf.at[q, :, own_shard], w_send, w_recv.at[q],
                    place(x, rem(y + k, 8), z, w_core),
                ).start()

            @pl.when(c == w_core)
            def _():
                local(w_ref.at[q], wbuf.at[q, :, own_shard], w_recv.at[q]).start()

            @pl.when(c != w_core)
            def _():
                remote(
                    w_ref.at[q], wbuf.at[q, :, own_shard], w_send, w_recv.at[q], place(x, y, z, w_core)
                ).start()

    def start_g(q):
        own = gbuf.at[q, :, c, own_rows]
        bytes_of(own, gload_sem.at[q])
        for k in range(1, 4):
            remote(own, own, g_send, g_recv.at[q], place(rem(x + k, 4), y, z, c)).start()

    for q in range(NQ):
        start_w(q)
        start_g(q)

    zero_rows = jnp.zeros((64, LANES), BF16)

    def clear(q, _):
        for arr in range(2):
            for image in range(2):
                gbuf[q, arr, image, 0:64, :] = zero_rows
                gbuf[q, arr, image, 576:640, :] = zero_rows
        return 0

    lax.fori_loop(0, NQ, clear, 0)
    for arr in range(2):
        acc[arr] = jnp.zeros((1152, 256), F32)

    bytes_of(vmain, v_recv)
    down, up = z_hi > 0, z_hi < 3
    at_down, at_up = place(x, y, rem(z + 6, 8), c), place(x, y, rem(z + 2, 8), c)
    vh_down = remote(vmain.at[:, 0:32], vhalo.at[:, 1], vh_send.at[0], vh_recv.at[0], at_down)
    vh_up = remote(vmain.at[:, 480:512], vhalo.at[:, 0], vh_send.at[1], vh_recv.at[1], at_up)

    @pl.when(down)
    def _():
        vh_down.start()

    @pl.when(up)
    def _():
        vh_up.start()

    column = lax.broadcasted_iota(jnp.int32, (128, 128), 0) & 31

    def turn(v, piece):
        taps = (
            jnp.where(column == 0, 0.0, pltpu.roll(v, 1, 0)),
            v,
            jnp.where(column == 31, 0.0, pltpu.roll(v, 127, 0)),
        )
        for tap in range(3):
            turned = taps[tap].T.astype(BF16)
            for arr in range(2):
                vt[arr, tap * 64 : tap * 64 + 64, 128 * piece : 128 * piece + 128] = turned[
                    arr * 64 : arr * 64 + 64
                ]

    for piece in range(8):
        turn(vmain[piece // 4, 128 * (piece % 4) : 128 * (piece % 4) + 128, :].astype(F32), piece)

    ahead = rem(z_lo + c, 2) == 0
    at_mate = place(x, y, rem(jnp.where(ahead, z + 1, z + 7), 8), c)
    at_twin = place(x, y, z, 1 - c)

    def forward_g(q):
        bytes_of(gbuf.at[q, :, c, 64:448], g_recv.at[q])
        ring_rows = gbuf.at[q, :, c, 64:576]
        remote(ring_rows, ring_rows, p_send, p_recv.at[q], at_twin).start()

    def forward_w(q):
        shards = wbuf.at[q, :, pl.ds(z_lo * 2, 2)]
        bytes_of(shards, w_recv.at[q])
        remote(shards, shards, wz_send, wz_recv.at[q], at_mate).start()

    def forward(q):
        forward_g(q)
        forward_w(q)

    forward(0)
    @pl.when(down)
    def _():
        vh_up.wait_recv()

    @pl.when(up)
    def _():
        vh_down.wait_recv()

    @pl.when(jnp.logical_not(down))
    def _():
        vhalo[:, 0] = jnp.zeros((2, 32, 128), BF16)

    @pl.when(jnp.logical_not(up))
    def _():
        vhalo[:, 1] = jnp.zeros((2, 32, 128), BF16)

    turn(vhalo[...].astype(F32).reshape(128, 128), 8)

    def sum_of(ref):
        value = ref[0].astype(F32)
        for k in range(1, 8):
            value = value + ref[k].astype(F32)
        return value.astype(BF16)

    def reduce_first(q):
        bytes_of(rs_in.at[q], rs_recv.at[q])
        a_out[q] = sum_of(rs_in.at[q])

        @pl.when(sums_y)
        def _():
            local(a_out.at[q], a_in.at[q, y], a_recv.at[q]).start()

        @pl.when(jnp.logical_not(sums_y))
        def _():
            remote(a_out.at[q], a_in.at[q, y], a_send, a_recv.at[q], place(x, block, z, c)).start()

        bytes_of(ry_in.at[q], ry_recv.at[q])
        ay_out[q] = sum_of(ry_in.at[q])
        z_to = 2 * q + div(y, 4)

        @pl.when(z_to == z)
        def _():
            local(ay_out.at[q], ay_in.at[z], ay_recv).start()

        @pl.when(z_to != z)
        def _():
            remote(ay_out.at[q], ay_in.at[z], ay_send, ay_recv, place(x, y, z_to, c)).start()

    def reduce_last_z():
        @pl.when(sums_z)
        def _():
            bytes_of(ay_in, ay_recv)
            cy_out[...] = sum_of(ay_in)

            @pl.when(own_y)
            def _():
                local(cy_out, cy_in.at[half_y], cy_recv).start()

            @pl.when(jnp.logical_not(own_y))
            def _():
                remote(cy_out, cy_in.at[half_y], cy_send, cy_recv, place(x, block, z, core_y)).start()

            for k in range(1, 4):
                remote(
                    cy_out, cy_in.at[half_y], cy_send, cy_recv, place(rem(x + k, 4), block, z, core_y)
                ).start()

    def reduce_y(quarter):
        @pl.when(sums_y)
        def _():
            bytes_of(a_in.at[quarter], a_recv.at[quarter])
            c_out[quarter] = sum_of(a_in.at[quarter])
            z_owner = 2 * quarter + z_lo
            mine = part_own & (z_owner == z)

            @pl.when(mine)
            def _():
                local(c_out.at[quarter], c_in.at[part_half], c_recv).start()

            @pl.when(jnp.logical_not(mine))
            def _():
                remote(
                    c_out.at[quarter], c_in.at[part_half], c_send, c_recv, place(x, y, z_owner, part_core)
                ).start()

            for k in range(1, 4):
                remote(
                    c_out.at[quarter], c_in.at[part_half], c_send, c_recv,
                    place(rem(x + k, 4), y, z_owner, part_core),
                ).start()

    def gather(q):
        kern = wbuf[q].reshape(192, 3 * LANES)
        windows = []
        for arr in range(2):
            views = []
            for image in range(2):
                views.append(
                    jnp.concatenate(
                        [gbuf[q, arr, image, 96 - 32 * a : 608 - 32 * a, :] for a in range(3)], axis=1
                    )
                )
            for image in range(2):
                for first in (64, 608):
                    views.append(
                        jnp.concatenate(
                            [gbuf[q, arr, image, first - 32 * a : first + 32 - 32 * a, :] for a in range(3)],
                            axis=1,
                        )
                    )
            windows.append(jnp.concatenate(views, axis=0))
        return kern, windows

    def back(q, kern, windows):
        for arr, factor in ((0, kern), (1, jnp.abs(kern))):
            acc[arr, :, 0:192] += lax.dot_general(
                windows[arr], factor, (((1,), (1,)), ((), ())), preferred_element_type=F32
            )

    def step(q, _):
        @pl.when(q < NQ - 1)
        def _():
            forward_w(q + 1)

        bytes_of(gbuf.at[q, :, 1 - c, 64:576], p_recv.at[q])
        bytes_of(wbuf.at[q, :, pl.ds((1 - z_lo) * 2, 2)], wz_recv.at[q])
        kern, windows = gather(q)
        terms = [jnp.dot(vt[arr], windows[arr], preferred_element_type=F32) for arr in range(2)]
        wide = kern.astype(F32)
        signed = jnp.where(wide > 0, terms[1], jnp.where(wide < 0, -terms[1], 0.0))
        partial = (terms[0] + signed).astype(BF16)

        def tile(tap_at, shard):
            a, tap = divmod(tap_at, 3)
            return partial[
                tap * 64 + shard * 16 : tap * 64 + shard * 16 + 16, a * 128 : a * 128 + 128
            ]

        for to in range(8):
            for k in range(3):
                rs_out[q, to, 16 * k : 16 * k + 16, :] = tile(2 * ((to // 2) % 2) + k, (to % 2) * 2 + to // 4)
        local(rs_out.at[q, z], rs_in.at[q, z], rs_recv.at[q]).start()
        for k in range(1, 8):
            zd = rem(z + k, 8)
            remote(rs_out.at[q, zd], rs_in.at[q, z], rs_send, rs_recv.at[q], place(x, y, zd, c)).start()
        for to in range(8):
            for k in range(2):
                ry_out[q, to, 16 * k : 16 * k + 16, :] = tile(5 + 2 * (to % 2) + k, to // 2)
        local(ry_out.at[q, y], ry_in.at[q, y], ry_recv.at[q]).start()
        for k in range(1, 8):
            yd = rem(y + k, 8)
            remote(ry_out.at[q, yd], ry_in.at[q, y], ry_send, ry_recv.at[q], place(x, yd, z, c)).start()

        @pl.when(q < NQ - 1)
        def _():
            forward_g(q + 1)

        back(q, kern, windows)

        @pl.when(q > 0)
        def _():
            reduce_first(q - 1)

        @pl.when(q > 1)
        def _():
            reduce_y(q - 2)
        return 0

    lax.fori_loop(0, NQ, step, 0)

    def late(q, _):
        back(q, *gather(q))
        return 0


    column64 = lax.broadcasted_iota(jnp.int32, (64, 128), 0) & 31
    low64 = lax.broadcasted_iota(jnp.int32, (64, 128), 1) < 64

    def fold(k, _):
        rows = pl.ds(mul(k * 64, 64), 64)
        c01, r01 = acc[0, rows, 0:128], acc[1, rows, 0:128]
        c2, r2 = acc[0, rows, 128:256], acc[1, rows, 128:256]
        first = jnp.where(low64, c01, pltpu.roll(r01, 64, 1))
        middle = jnp.where(low64, pltpu.roll(c01, 64, 1), r01)
        last = jnp.where(low64, c2, pltpu.roll(r2, 64, 1))
        value = (
            middle
            + jnp.where(column64 == 31, 0.0, pltpu.roll(first, 63, 0))
            + jnp.where(column64 == 0, 0.0, pltpu.roll(last, 1, 0))
        )
        total[rows, :] = value
        return 0

    lax.fori_loop(16, 18, fold, 0)
    for image in range(2):
        for side in range(2):
            first = 1024 + 64 * image + 32 * side
            halo_out[side, image] = total[first : first + 32, :]
    h_down = remote(halo_out.at[0], halo_in.at[0], h_send.at[0], h_recv.at[0], at_down)
    h_up = remote(halo_out.at[1], halo_in.at[1], h_send.at[1], h_recv.at[1], at_up)

    @pl.when(down)
    def _():
        h_down.start()

    @pl.when(up)
    def _():
        h_up.start()

    lax.fori_loop(0, 16, fold, 0)
    for image in range(2):
        r_out[image] = total[512 * image : 512 * image + 512, :].astype(BF16)

    def r_start(b):
        @pl.when(b == block)
        def _():
            local(r_out.at[c, pl.ds(mul(128 * x, 128), 128)], r_in.at[block], r_recv).start()

        @pl.when(b != block)
        def _():
            remote(
                r_out.at[b // 4, 128 * (b % 4) : 128 * (b % 4) + 128], r_in.at[block], r_send, r_recv,
                place(b % 4, y, z, b // 4),
            ).start()

    for b in (1, 2, 5, 6):
        r_start(b)
    reduce_y(NQ - 2)
    reduce_first(NQ - 1)

    @pl.when(up)
    def _():
        h_down.wait_recv()
        for image in range(2):
            r_out[image, 480:512, :] = (total[512 * image + 480 : 512 * image + 512, :] + halo_in[0, image]).astype(BF16)

    @pl.when(down)
    def _():
        h_up.wait_recv()
        for image in range(2):
            r_out[image, 0:32, :] = (total[512 * image : 512 * image + 32, :] + halo_in[1, image]).astype(BF16)

    for b in (0, 3, 4, 7):
        r_start(b)

    reduce_y(NQ - 1)
    reduce_last_z()

    bytes_of(r_in, r_recv)
    for j in range(4):
        lanes = slice(128 * j, 128 * j + 128)
        even, odd = r_in[2 * j].astype(F32), r_in[2 * j + 1].astype(F32)
        center = jnp.where(low, even, pltpu.roll(odd, 64, 1))
        radius = jnp.where(low, pltpu.roll(even, 64, 1), odd)
        cm_out[:, lanes], rm_out[:, lanes] = center.astype(BF16), radius.astype(BF16)

    bytes_of(vsend.at[0:7], v_send)
    bytes_of(r_in.at[0:7], r_send)

    @pl.when(down)
    def _():
        vh_down.wait_send()
        h_down.wait_send()

    @pl.when(up)
    def _():
        vh_up.wait_send()
        h_up.wait_send()

    bytes_of(gbuf.at[:, :, c, 64:448], g_send)
    bytes_of(gbuf.at[:, :, c, 64:576], p_send)
    bytes_of(wbuf.at[:, :, pl.ds(z_lo * 2, 2)], wz_send)

    @pl.when(w_source & (c == w_core))
    def _():
        bytes_of(acc.at[0, 0:1008], w_send)

    @pl.when(w_source & (c != w_core))
    def _():
        bytes_of(acc.at[0], w_send)

    bytes_of(rs_out.at[:, 0:7], rs_send)
    bytes_of(ry_out.at[:, 0:7], ry_send)

    @pl.when(jnp.logical_not(sums_y))
    def _():
        bytes_of(a_out, a_send)

    @pl.when(sums_z)
    def _():
        bytes_of(ay_out.at[0:3], ay_send)

    @pl.when(jnp.logical_not(sums_z))
    def _():
        bytes_of(ay_out, ay_send)

    @pl.when(sums_z & own_y)
    def _():
        bytes_of(ay_in.at[0:3], cy_send)

    @pl.when(sums_z & jnp.logical_not(own_y))
    def _():
        bytes_of(ay_in.at[0:4], cy_send)

    @pl.when(sums_y & part_own)
    def _():
        bytes_of(a_in.at[0:3, 0:5], c_send)

    @pl.when(sums_y & jnp.logical_not(part_own))
    def _():
        bytes_of(a_in.at[0:2], c_send)

    bytes_of(c_in, c_recv)
    bytes_of(cy_in, cy_recv)
    for rows, value in (
        ((0, 48), c_in[0]), ((48, 80), c_in[1, 16:48]), ((80, 112), cy_in[0]), ((112, 144), cy_in[1]),
    ):
        wg_out[rows[0] : rows[1], :] = value.astype(F32) * (1.0 / 32.0)


def on_device(center_mid, radius_mid, conv_weight, center_upstream, radius_upstream):
    flat = [v.reshape(128, 512) for v in (center_mid, radius_mid, center_upstream, radius_upstream)]
    weight = conv_weight.reshape(16, 3, 3, NQ, LANES).transpose(3, 2, 0, 1, 4)
    weight = weight.reshape(NQ, 3, 16, 3 * LANES)
    dma = pltpu.SemaphoreType.DMA
    hbm, vmem = pl.BlockSpec(memory_space=pltpu.HBM), pl.BlockSpec(memory_space=pltpu.VMEM)
    center_grad, radius_grad, weight_grad = pl.pallas_call(
        kernel,
        out_shape=(
            jax.ShapeDtypeStruct((128, 512), BF16),
            jax.ShapeDtypeStruct((128, 512), BF16),
            jax.ShapeDtypeStruct((144, 128), F32),
        ),
        in_specs=[hbm, hbm, hbm, hbm, vmem],
        out_specs=(vmem, vmem, vmem),
        scratch_shapes=[
            pltpu.VMEM((128, 512), BF16),
            pltpu.VMEM((128, 512), BF16),
            pltpu.VMEM((8, 128, 128), BF16),
            pltpu.VMEM((2, 512, 128), BF16),
            pltpu.VMEM((2, 2, 32, 128), BF16),
            pltpu.VMEM((2, 192, 1152), BF16),
            pltpu.VMEM((NQ, 2, 2, 640, LANES), BF16),
            pltpu.VMEM((NQ, 3, 4, 16, 3 * LANES), BF16),
            pltpu.VMEM((2, 1152, 256), F32),
            pltpu.VMEM((4, 8, 48, 128), BF16),
            pltpu.VMEM((4, 8, 48, 128), BF16),
            pltpu.VMEM((4, 8, 32, 128), BF16),
            pltpu.VMEM((4, 8, 32, 128), BF16),
            pltpu.VMEM((4, 48, 128), BF16),
            pltpu.VMEM((4, 8, 48, 128), BF16),
            pltpu.VMEM((4, 32, 128), BF16),
            pltpu.VMEM((8, 32, 128), BF16),
            pltpu.VMEM((4, 48, 128), BF16),
            pltpu.VMEM((2, 48, 128), BF16),
            pltpu.VMEM((32, 128), BF16),
            pltpu.VMEM((2, 32, 128), BF16),
            pltpu.VMEM((2, 2, 32, 128), F32),
            pltpu.VMEM((2, 2, 32, 128), F32),
            pltpu.VMEM((1152, 128), F32),
            pltpu.VMEM((2, 512, 128), BF16),
            pltpu.VMEM((8, 128, 128), BF16),
            dma((2,)), dma((NQ,)), dma, dma, dma((2,)), dma((2,)), dma, dma((NQ,)), dma, dma((NQ,)),
            dma, dma((NQ,)), dma, dma((NQ,)), dma, dma((NQ,)), dma, dma((NQ,)), dma, dma((4,)), dma, dma,
            dma, dma, dma, dma,
            dma((2,)), dma((2,)), dma, dma,
        ],
        compiler_params=pltpu.CompilerParams(
            collective_id=0, has_side_effects=True, vmem_limit_bytes=48 << 20
        ),
    )(flat[0], flat[1], flat[2], flat[3], weight)
    middle, spread = flat[0].astype(F32), flat[1].astype(F32)
    center, radius = center_grad.astype(F32), radius_grad.astype(F32)
    upper = jnp.where(middle > -spread, 0.5 * (center + radius), 0.0)
    lower = jnp.where(middle > spread, 0.5 * (center - radius), 0.0)
    center_grad, radius_grad = (upper + lower).astype(BF16), (upper - lower).astype(BF16)
    x = lax.rem(lax.axis_index("rows"), 4)
    own = lax.dynamic_slice_in_dim(weight_grad, x * 32, 32, axis=1)
    return (
        center_grad.reshape(center_mid.shape),
        radius_grad.reshape(center_mid.shape),
        own.reshape(3, 3, 16, 32).transpose(2, 0, 1, 3),
    )


def solution(mesh):
    placed = (
        P("img", "rows", None, None),
        P("img", "rows", None, None),
        P("img", None, None, None),
        P("img", "rows", None, None),
        P("img", "rows", None, None),
    )
    return jax.shard_map(
        on_device,
        mesh=mesh,
        in_specs=placed,
        out_specs=(
            P("img", "rows", None, None),
            P("img", "rows", None, None),
            P("img", None, None, "rows"),
        ),
        check_vma=False,
    )
```

```python
import jax
import jax.numpy as jnp
from jax import lax
from jax.experimental import pallas as pl
from jax.experimental.pallas import tpu as pltpu
from jax.sharding import PartitionSpec as P

MESH = pl.DeviceIdType.MESH
F32 = jnp.float32
BF16 = jnp.bfloat16
LAG = 2
FAR = (4, 3, 5, 2, 6, 1, 7)
NQ = 4
LANES = 512 // NQ
QB = 4 // NQ


def rem(value, by):
    return lax.rem(value, jnp.int32(by))


def div(value, by):
    return lax.div(value, jnp.int32(by))


def place(x, y, z, c):
    return ((y * 2 + rem(z, 2)) * 2 + c, div(z, 2) * 4 + x)


def remote(src, dst, send, recv, where):
    return pltpu.make_async_remote_copy(
        src_ref=src, dst_ref=dst, send_sem=send, recv_sem=recv, device_id=where, device_id_type=MESH
    )


def local(src, dst, sem):
    return pltpu.make_async_copy(src, dst, sem)


def bytes_of(ref, sem):
    pltpu.make_async_copy(ref, ref, sem).wait()


def mul(value, by):
    return pl.multiple_of(value, by)


def kernel(
    cm_hbm, rm_hbm, gc_hbm, gr_hbm, w_ref,
    cm_out, rm_out, wg_out,
    cm, rm, vsend, vmain, vhalo, vt, gbuf, wbuf, acc, rs_out, rs_in, ry_out, ry_in, a_out, a_in, ay_out, ay_in, c_out, c_in, cy_out, cy_in,
    halo_out, halo_in, total, r_out, r_in,
    load_sem, gload_sem, v_send, v_recv, vh_send, vh_recv, g_send, g_recv, p_send, p_recv,
    w_send, w_recv, wz_send, wz_recv, rs_send, rs_recv, ry_send, ry_recv, a_send, a_recv, ay_send, ay_recv, c_send, c_recv, cy_send, cy_recv,
    h_send, h_recv, r_send, r_recv,
):
    i_img, i_rows = lax.axis_index("img"), lax.axis_index("rows")
    x, z_hi = rem(i_rows, 4), div(i_rows, 4)
    y, z_lo, c = div(i_img, 4), rem(div(i_img, 2), 2), rem(i_img, 2)
    z = z_hi * 2 + z_lo
    block = x + 4 * c
    w_source = rem(y, 4) == x
    w_core = div(y, 4)
    part_core, part_half = div(z, 4), rem(div(z, 2), 2)
    sums_y = y == block
    part_own = part_core == c
    sums_z = z_lo == div(y, 4)
    core_y, half_y = rem(div(y, 2), 2), rem(y, 2)
    own_y = (y == block) & (core_y == c)

    barrier = pltpu.get_barrier_semaphore()

    def greet(where):
        pl.semaphore_signal(barrier, inc=1, device_id=where, device_id_type=MESH)

    for k in FAR:
        greet(place(rem(x + k, 4), y, z, rem(c + k // 4, 2)))
        greet(place(x, y, rem(z + k, 8), c))
        greet(place(x, rem(y + k, 8), z, c))
    greet(place(x, block, z, 1 - c))
    for half in range(2):
        xs, zs, cs = rem(y, 4), 2 * (2 * c + half) + z_lo, div(y, 4)
        same = (xs == x) & (zs == z) & (cs == c)

        @pl.when(jnp.logical_not(same))
        def _():
            greet(place(xs, y, zs, cs))

        ys = 4 * z_lo + 2 * c + half
        same_y = (xs == x) & (ys == y) & (cs == c)

        @pl.when(jnp.logical_not(same_y))
        def _():
            greet(place(xs, ys, z, cs))

    expected = (
        21
        + jnp.where(sums_z, 4 - jnp.where(own_y, 1, 0), 0)
        + jnp.where(w_source & (c != w_core), 8, 0)
        + jnp.where(sums_y, 16 - jnp.where(part_own, 1, 0), 0)
    )

    load_cm = local(cm_hbm, cm, load_sem.at[0])
    load_rm = local(rm_hbm, rm, load_sem.at[1])
    load_cm.start()
    load_rm.start()
    own_rows = pl.ds(mul(64 + 128 * x, 64), 128)
    for q in range(NQ):
        for arr, ref in ((0, gc_hbm), (1, gr_hbm)):
            local(
                ref.at[:, LANES * q : LANES * q + LANES], gbuf.at[q, arr, c, own_rows], gload_sem.at[q]
            ).start()

    load_cm.wait()
    load_rm.wait()
    lane = lax.broadcasted_iota(jnp.int32, (128, 128), 1)
    low = lane < 64
    for j in range(4):
        middle = cm[:, 128 * j : 128 * j + 128].astype(F32)
        spread = rm[:, 128 * j : 128 * j + 128].astype(F32)
        upper = jnp.maximum(middle + spread, 0.0)
        lower = jnp.maximum(middle - spread, 0.0)
        center = (upper + lower) * 0.5
        radius = (upper - lower) * 0.5
        vsend[2 * j] = jnp.where(low, center, pltpu.roll(radius, 64, 1)).astype(BF16)
        vsend[2 * j + 1] = jnp.where(low, pltpu.roll(center, 64, 1), radius).astype(BF16)

    pl.semaphore_wait(barrier, expected)

    own_shard = z_lo * 2 + c

    def start_w(q):
        @pl.when(w_source)
        def _():
            for k in FAR:
                remote(
                    w_ref.at[q], wbuf.at[q, :, own_shard], w_send, w_recv.at[q],
                    place(x, rem(y + k, 8), z, w_core),
                ).start()

            @pl.when(c == w_core)
            def _():
                local(w_ref.at[q], wbuf.at[q, :, own_shard], w_recv.at[q]).start()

            @pl.when(c != w_core)
            def _():
                remote(
                    w_ref.at[q], wbuf.at[q, :, own_shard], w_send, w_recv.at[q], place(x, y, z, w_core)
                ).start()

    def start_g(q):
        own = gbuf.at[q, :, c, own_rows]
        bytes_of(own, gload_sem.at[q])
        for k in (2, 1, 3):
            remote(own, own, g_send, g_recv.at[q], place(rem(x + k, 4), y, z, c)).start()

    start_w(0)
    v_place = vmain.at[c, pl.ds(mul(128 * x, 128), 128)]
    for k in (2, 6, 1, 3, 5, 7, 4):
        xd, cd = rem(x + k, 4), rem(c + k // 4, 2)
        remote(vsend.at[xd + 4 * cd], v_place, v_send, v_recv, place(xd, y, z, cd)).start()
    local(vsend.at[block], v_place, v_recv).start()
    for q in range(NQ):
        if q > 0:
            start_w(q)
        start_g(q)

    zero_rows = jnp.zeros((64, LANES), BF16)

    def clear(q, _):
        for arr in range(2):
            for image in range(2):
                gbuf[q, arr, image, 0:64, :] = zero_rows
                gbuf[q, arr, image, 576:640, :] = zero_rows
        return 0

    lax.fori_loop(0, NQ, clear, 0)
    for arr in range(2):
        acc[arr] = jnp.zeros((1152, 256), F32)

    bytes_of(vmain, v_recv)
    down, up = z_hi > 0, z_hi < 3
    at_down, at_up = place(x, y, rem(z + 6, 8), c), place(x, y, rem(z + 2, 8), c)
    vh_down = remote(vmain.at[:, 0:32], vhalo.at[:, 1], vh_send.at[0], vh_recv.at[0], at_down)
    vh_up = remote(vmain.at[:, 480:512], vhalo.at[:, 0], vh_send.at[1], vh_recv.at[1], at_up)

    @pl.when(down)
    def _():
        vh_down.start()

    @pl.when(up)
    def _():
        vh_up.start()

    column = lax.broadcasted_iota(jnp.int32, (128, 128), 0) & 31

    def turn(v, piece):
        taps = (
            jnp.where(column == 0, 0.0, pltpu.roll(v, 1, 0)),
            v,
            jnp.where(column == 31, 0.0, pltpu.roll(v, 127, 0)),
        )
        for tap in range(3):
            turned = taps[tap].T.astype(BF16)
            for arr in range(2):
                vt[arr, tap * 64 : tap * 64 + 64, 128 * piece : 128 * piece + 128] = turned[
                    arr * 64 : arr * 64 + 64
                ]

    for piece in range(8):
        turn(vmain[piece // 4, 128 * (piece % 4) : 128 * (piece % 4) + 128, :].astype(F32), piece)

    ahead = rem(z_lo + c, 2) == 0
    at_mate = place(x, y, rem(jnp.where(ahead, z + 1, z + 7), 8), c)
    at_twin = place(x, y, z, 1 - c)

    def forward_g(q):
        bytes_of(gbuf.at[q, :, c, 64:448], g_recv.at[q])
        ring_rows = gbuf.at[q, :, c, 64:576]
        remote(ring_rows, ring_rows, p_send, p_recv.at[q], at_twin).start()

    def forward_w(q):
        shards = wbuf.at[q, :, pl.ds(z_lo * 2, 2)]
        bytes_of(shards, w_recv.at[q])
        remote(shards, shards, wz_send, wz_recv.at[q], at_mate).start()

    forward_g(0)
    forward_w(0)
    forward_w(1)
    @pl.when(down)
    def _():
        vh_up.wait_recv()

    @pl.when(up)
    def _():
        vh_down.wait_recv()

    @pl.when(jnp.logical_not(down))
    def _():
        vhalo[:, 0] = jnp.zeros((2, 32, 128), BF16)

    @pl.when(jnp.logical_not(up))
    def _():
        vhalo[:, 1] = jnp.zeros((2, 32, 128), BF16)

    turn(vhalo[...].astype(F32).reshape(128, 128), 8)

    def sum_of(ref):
        value = ref[0].astype(F32)
        for k in range(1, 8):
            value = value + ref[k].astype(F32)
        return value.astype(BF16)

    def reduce_first(q):
        bytes_of(rs_in.at[q], rs_recv.at[q])
        a_out[q] = sum_of(rs_in.at[q])

        @pl.when(sums_y)
        def _():
            local(a_out.at[q], a_in.at[q, y], a_recv.at[q]).start()

        @pl.when(jnp.logical_not(sums_y))
        def _():
            remote(a_out.at[q], a_in.at[q, y], a_send, a_recv.at[q], place(x, block, z, c)).start()

        bytes_of(ry_in.at[q], ry_recv.at[q])
        ay_out[q] = sum_of(ry_in.at[q])
        z_to = 2 * q + div(y, 4)

        @pl.when(z_to == z)
        def _():
            local(ay_out.at[q], ay_in.at[z], ay_recv).start()

        @pl.when(z_to != z)
        def _():
            remote(ay_out.at[q], ay_in.at[z], ay_send, ay_recv, place(x, y, z_to, c)).start()

    def reduce_last_z():
        @pl.when(sums_z)
        def _():
            bytes_of(ay_in, ay_recv)
            cy_out[...] = sum_of(ay_in)

            @pl.when(own_y)
            def _():
                local(cy_out, cy_in.at[half_y], cy_recv).start()

            @pl.when(jnp.logical_not(own_y))
            def _():
                remote(cy_out, cy_in.at[half_y], cy_send, cy_recv, place(x, block, z, core_y)).start()

            for k in range(1, 4):
                remote(
                    cy_out, cy_in.at[half_y], cy_send, cy_recv, place(rem(x + k, 4), block, z, core_y)
                ).start()

    def reduce_y(quarter):
        @pl.when(sums_y)
        def _():
            bytes_of(a_in.at[quarter], a_recv.at[quarter])
            c_out[quarter] = sum_of(a_in.at[quarter])
            z_owner = 2 * quarter + z_lo
            mine = part_own & (z_owner == z)

            @pl.when(mine)
            def _():
                local(c_out.at[quarter], c_in.at[part_half], c_recv).start()

            @pl.when(jnp.logical_not(mine))
            def _():
                remote(
                    c_out.at[quarter], c_in.at[part_half], c_send, c_recv, place(x, y, z_owner, part_core)
                ).start()

            for k in range(1, 4):
                remote(
                    c_out.at[quarter], c_in.at[part_half], c_send, c_recv,
                    place(rem(x + k, 4), y, z_owner, part_core),
                ).start()

    def gather(q):
        kern = wbuf[q].reshape(192, 3 * LANES)
        windows = []
        for arr in range(2):
            views = []
            for image in range(2):
                views.append(
                    jnp.concatenate(
                        [gbuf[q, arr, image, 96 - 32 * a : 608 - 32 * a, :] for a in range(3)], axis=1
                    )
                )
            for image in range(2):
                for first in (64, 608):
                    views.append(
                        jnp.concatenate(
                            [gbuf[q, arr, image, first - 32 * a : first + 32 - 32 * a, :] for a in range(3)],
                            axis=1,
                        )
                    )
            windows.append(jnp.concatenate(views, axis=0))
        return kern, windows

    def back(q, kern, windows):
        for arr, factor in ((0, kern), (1, jnp.abs(kern))):
            acc[arr, :, 0:192] += lax.dot_general(
                windows[arr], factor, (((1,), (1,)), ((), ())), preferred_element_type=F32
            )

    def step(q, _):
        @pl.when(q < NQ - 2)
        def _():
            forward_w(q + 2)

        bytes_of(gbuf.at[q, :, 1 - c, 64:576], p_recv.at[q])
        bytes_of(wbuf.at[q, :, pl.ds((1 - z_lo) * 2, 2)], wz_recv.at[q])
        kern, windows = gather(q)
        terms = [jnp.dot(vt[arr], windows[arr], preferred_element_type=F32) for arr in range(2)]
        wide = kern.astype(F32)
        signed = jnp.where(wide > 0, terms[1], jnp.where(wide < 0, -terms[1], 0.0))
        partial = (terms[0] + signed).astype(BF16)

        def tile(tap_at, shard):
            a, tap = divmod(tap_at, 3)
            return partial[
                tap * 64 + shard * 16 : tap * 64 + shard * 16 + 16, a * 128 : a * 128 + 128
            ]

        for to in range(8):
            for k in range(3):
                rs_out[q, to, 16 * k : 16 * k + 16, :] = tile(2 * ((to // 2) % 2) + k, (to % 2) * 2 + to // 4)
        local(rs_out.at[q, z], rs_in.at[q, z], rs_recv.at[q]).start()
        for k in FAR:
            zd = rem(z + k, 8)
            remote(rs_out.at[q, zd], rs_in.at[q, z], rs_send, rs_recv.at[q], place(x, y, zd, c)).start()
        for to in range(8):
            for k in range(2):
                ry_out[q, to, 16 * k : 16 * k + 16, :] = tile(5 + 2 * (to % 2) + k, to // 2)
        local(ry_out.at[q, y], ry_in.at[q, y], ry_recv.at[q]).start()
        for k in FAR:
            yd = rem(y + k, 8)
            remote(ry_out.at[q, yd], ry_in.at[q, y], ry_send, ry_recv.at[q], place(x, yd, z, c)).start()

        @pl.when(q < NQ - 1)
        def _():
            forward_g(q + 1)

        back(q, kern, windows)

        @pl.when(q >= LAG)
        def _():
            reduce_first(q - LAG)

        @pl.when(q >= LAG + 1)
        def _():
            reduce_y(q - LAG - 1)
        return 0

    lax.fori_loop(0, NQ, step, 0)

    column64 = lax.broadcasted_iota(jnp.int32, (64, 128), 0) & 31
    low64 = lax.broadcasted_iota(jnp.int32, (64, 128), 1) < 64

    def fold(k, _):
        rows = pl.ds(mul(k * 64, 64), 64)
        c01, r01 = acc[0, rows, 0:128], acc[1, rows, 0:128]
        c2, r2 = acc[0, rows, 128:256], acc[1, rows, 128:256]
        first = jnp.where(low64, c01, pltpu.roll(r01, 64, 1))
        middle = jnp.where(low64, pltpu.roll(c01, 64, 1), r01)
        last = jnp.where(low64, c2, pltpu.roll(r2, 64, 1))
        value = (
            middle
            + jnp.where(column64 == 31, 0.0, pltpu.roll(first, 63, 0))
            + jnp.where(column64 == 0, 0.0, pltpu.roll(last, 1, 0))
        )
        total[rows, :] = value
        return 0

    lax.fori_loop(16, 18, fold, 0)
    for image in range(2):
        for side in range(2):
            first = 1024 + 64 * image + 32 * side
            halo_out[side, image] = total[first : first + 32, :]
    h_down = remote(halo_out.at[0], halo_in.at[0], h_send.at[0], h_recv.at[0], at_down)
    h_up = remote(halo_out.at[1], halo_in.at[1], h_send.at[1], h_recv.at[1], at_up)

    @pl.when(down)
    def _():
        h_down.start()

    @pl.when(up)
    def _():
        h_up.start()

    lax.fori_loop(0, 16, fold, 0)
    for image in range(2):
        r_out[image] = total[512 * image : 512 * image + 512, :].astype(BF16)

    def r_start(b):
        @pl.when(b == block)
        def _():
            local(r_out.at[c, pl.ds(mul(128 * x, 128), 128)], r_in.at[block], r_recv).start()

        @pl.when(b != block)
        def _():
            remote(
                r_out.at[b // 4, 128 * (b % 4) : 128 * (b % 4) + 128], r_in.at[block], r_send, r_recv,
                place(b % 4, y, z, b // 4),
            ).start()

    for b in (1, 2, 5, 6):
        r_start(b)
    for q in range(NQ - LAG, NQ):
        reduce_first(q)
        reduce_y(q - 1)

    @pl.when(up)
    def _():
        h_down.wait_recv()
        for image in range(2):
            r_out[image, 480:512, :] = (total[512 * image + 480 : 512 * image + 512, :] + halo_in[0, image]).astype(BF16)

    @pl.when(down)
    def _():
        h_up.wait_recv()
        for image in range(2):
            r_out[image, 0:32, :] = (total[512 * image : 512 * image + 32, :] + halo_in[1, image]).astype(BF16)

    for b in (0, 3, 4, 7):
        r_start(b)

    reduce_y(NQ - 1)
    reduce_last_z()

    bytes_of(r_in, r_recv)
    for j in range(4):
        lanes = slice(128 * j, 128 * j + 128)
        even, odd = r_in[2 * j].astype(F32), r_in[2 * j + 1].astype(F32)
        center = jnp.where(low, even, pltpu.roll(odd, 64, 1))
        radius = jnp.where(low, pltpu.roll(even, 64, 1), odd)
        cm_out[:, lanes], rm_out[:, lanes] = center.astype(BF16), radius.astype(BF16)

    bytes_of(vsend.at[0:7], v_send)
    bytes_of(r_in.at[0:7], r_send)

    @pl.when(down)
    def _():
        vh_down.wait_send()
        h_down.wait_send()

    @pl.when(up)
    def _():
        vh_up.wait_send()
        h_up.wait_send()

    bytes_of(gbuf.at[:, :, c, 64:448], g_send)
    bytes_of(gbuf.at[:, :, c, 64:576], p_send)
    bytes_of(wbuf.at[:, :, pl.ds(z_lo * 2, 2)], wz_send)

    @pl.when(w_source & (c == w_core))
    def _():
        bytes_of(acc.at[0, 0:1008], w_send)

    @pl.when(w_source & (c != w_core))
    def _():
        bytes_of(acc.at[0], w_send)

    bytes_of(rs_out.at[:, 0:7], rs_send)
    bytes_of(ry_out.at[:, 0:7], ry_send)

    @pl.when(jnp.logical_not(sums_y))
    def _():
        bytes_of(a_out, a_send)

    @pl.when(sums_z)
    def _():
        bytes_of(ay_out.at[0:3], ay_send)

    @pl.when(jnp.logical_not(sums_z))
    def _():
        bytes_of(ay_out, ay_send)

    @pl.when(sums_z & own_y)
    def _():
        bytes_of(ay_in.at[0:3], cy_send)

    @pl.when(sums_z & jnp.logical_not(own_y))
    def _():
        bytes_of(ay_in.at[0:4], cy_send)

    @pl.when(sums_y & part_own)
    def _():
        bytes_of(a_in.at[0:3, 0:5], c_send)

    @pl.when(sums_y & jnp.logical_not(part_own))
    def _():
        bytes_of(a_in.at[0:2], c_send)

    bytes_of(c_in, c_recv)
    bytes_of(cy_in, cy_recv)
    for rows, value in (
        ((0, 48), c_in[0]), ((48, 80), c_in[1, 16:48]), ((80, 112), cy_in[0]), ((112, 144), cy_in[1]),
    ):
        wg_out[rows[0] : rows[1], :] = value.astype(F32) * (1.0 / 32.0)


def on_device(center_mid, radius_mid, conv_weight, center_upstream, radius_upstream):
    flat = [v.reshape(128, 512) for v in (center_mid, radius_mid, center_upstream, radius_upstream)]
    weight = conv_weight.reshape(16, 3, 3, NQ, LANES).transpose(3, 2, 0, 1, 4)
    weight = weight.reshape(NQ, 3, 16, 3 * LANES)
    dma = pltpu.SemaphoreType.DMA
    hbm, vmem = pl.BlockSpec(memory_space=pltpu.HBM), pl.BlockSpec(memory_space=pltpu.VMEM)
    center_grad, radius_grad, weight_grad = pl.pallas_call(
        kernel,
        out_shape=(
            jax.ShapeDtypeStruct((128, 512), BF16),
            jax.ShapeDtypeStruct((128, 512), BF16),
            jax.ShapeDtypeStruct((144, 128), F32),
        ),
        in_specs=[hbm, hbm, hbm, hbm, vmem],
        out_specs=(vmem, vmem, vmem),
        scratch_shapes=[
            pltpu.VMEM((128, 512), BF16),
            pltpu.VMEM((128, 512), BF16),
            pltpu.VMEM((8, 128, 128), BF16),
            pltpu.VMEM((2, 512, 128), BF16),
            pltpu.VMEM((2, 2, 32, 128), BF16),
            pltpu.VMEM((2, 192, 1152), BF16),
            pltpu.VMEM((NQ, 2, 2, 640, LANES), BF16),
            pltpu.VMEM((NQ, 3, 4, 16, 3 * LANES), BF16),
            pltpu.VMEM((2, 1152, 256), F32),
            pltpu.VMEM((4, 8, 48, 128), BF16),
            pltpu.VMEM((4, 8, 48, 128), BF16),
            pltpu.VMEM((4, 8, 32, 128), BF16),
            pltpu.VMEM((4, 8, 32, 128), BF16),
            pltpu.VMEM((4, 48, 128), BF16),
            pltpu.VMEM((4, 8, 48, 128), BF16),
            pltpu.VMEM((4, 32, 128), BF16),
            pltpu.VMEM((8, 32, 128), BF16),
            pltpu.VMEM((4, 48, 128), BF16),
            pltpu.VMEM((2, 48, 128), BF16),
            pltpu.VMEM((32, 128), BF16),
            pltpu.VMEM((2, 32, 128), BF16),
            pltpu.VMEM((2, 2, 32, 128), F32),
            pltpu.VMEM((2, 2, 32, 128), F32),
            pltpu.VMEM((1152, 128), F32),
            pltpu.VMEM((2, 512, 128), BF16),
            pltpu.VMEM((8, 128, 128), BF16),
            dma((2,)), dma((NQ,)), dma, dma, dma((2,)), dma((2,)), dma, dma((NQ,)), dma, dma((NQ,)),
            dma, dma((NQ,)), dma, dma((NQ,)), dma, dma((NQ,)), dma, dma((NQ,)), dma, dma((4,)), dma, dma,
            dma, dma, dma, dma,
            dma((2,)), dma((2,)), dma, dma,
        ],
        compiler_params=pltpu.CompilerParams(
            collective_id=0, has_side_effects=True, vmem_limit_bytes=48 << 20
        ),
    )(flat[0], flat[1], flat[2], flat[3], weight)
    middle, spread = flat[0].astype(F32), flat[1].astype(F32)
    center, radius = center_grad.astype(F32), radius_grad.astype(F32)
    upper = jnp.where(middle > -spread, 0.5 * (center + radius), 0.0)
    lower = jnp.where(middle > spread, 0.5 * (center - radius), 0.0)
    center_grad, radius_grad = (upper + lower).astype(BF16), (upper - lower).astype(BF16)
    x = lax.rem(lax.axis_index("rows"), 4)
    own = lax.dynamic_slice_in_dim(weight_grad, x * 32, 32, axis=1)
    return (
        center_grad.reshape(center_mid.shape),
        radius_grad.reshape(center_mid.shape),
        own.reshape(3, 3, 16, 32).transpose(2, 0, 1, 3),
    )


def solution(mesh):
    placed = (
        P("img", "rows", None, None),
        P("img", "rows", None, None),
        P("img", None, None, None),
        P("img", "rows", None, None),
        P("img", "rows", None, None),
    )
    return jax.shard_map(
        on_device,
        mesh=mesh,
        in_specs=placed,
        out_specs=(
            P("img", "rows", None, None),
            P("img", "rows", None, None),
            P("img", None, None, "rows"),
        ),
        check_vma=False,
    )
```

```python
import jax
import jax.numpy as jnp
from jax import lax
from jax.experimental import pallas as pl
from jax.experimental.pallas import tpu as pltpu
from jax.sharding import PartitionSpec as P

MESH = pl.DeviceIdType.MESH
F32 = jnp.float32
BF16 = jnp.bfloat16
LAG = 2
FAR = (4, 3, 5, 2, 6, 1, 7)
NQ = 4
LANES = 512 // NQ
QB = 4 // NQ


def rem(value, by):
    return lax.rem(value, jnp.int32(by))


def div(value, by):
    return lax.div(value, jnp.int32(by))


def place(x, y, z, c):
    return ((y * 2 + rem(z, 2)) * 2 + c, div(z, 2) * 4 + x)


def remote(src, dst, send, recv, where):
    return pltpu.make_async_remote_copy(
        src_ref=src, dst_ref=dst, send_sem=send, recv_sem=recv, device_id=where, device_id_type=MESH
    )


def local(src, dst, sem):
    return pltpu.make_async_copy(src, dst, sem)


def bytes_of(ref, sem):
    pltpu.make_async_copy(ref, ref, sem).wait()


def mul(value, by):
    return pl.multiple_of(value, by)


def kernel(
    cm_hbm, rm_hbm, gc_hbm, gr_hbm, w_ref,
    cm_out, rm_out, wg_out,
    cm, rm, vsend, vmain, vhalo, vt, gbuf, wbuf, acc, rs_out, rs_in, ry_out, ry_in, a_out, a_in, ay_out, ay_in, c_out, c_in, cy_out, cy_in,
    halo_out, halo_in, total, r_out, r_in,
    load_sem, gload_sem, v_send, v_recv, vh_send, vh_recv, g_send, g_recv, p_send, p_recv,
    w_send, w_recv, wz_send, wz_recv, rs_send, rs_recv, ry_send, ry_recv, a_send, a_recv, ay_send, ay_recv, c_send, c_recv, cy_send, cy_recv,
    h_send, h_recv, r_send, r_recv,
):
    i_img, i_rows = lax.axis_index("img"), lax.axis_index("rows")
    x, z_hi = rem(i_rows, 4), div(i_rows, 4)
    y, z_lo, c = div(i_img, 4), rem(div(i_img, 2), 2), rem(i_img, 2)
    z = z_hi * 2 + z_lo
    block = x + 4 * c
    w_source = rem(y, 4) == x
    w_core = div(y, 4)
    part_core, part_half = div(z, 4), rem(div(z, 2), 2)
    sums_y = y == block
    part_own = part_core == c
    sums_z = z_lo == div(y, 4)
    core_y, half_y = rem(div(y, 2), 2), rem(y, 2)
    own_y = (y == block) & (core_y == c)

    barrier = pltpu.get_barrier_semaphore()

    def greet(where):
        pl.semaphore_signal(barrier, inc=1, device_id=where, device_id_type=MESH)

    for k in FAR:
        greet(place(rem(x + k, 4), y, z, rem(c + k // 4, 2)))
        greet(place(x, y, rem(z + k, 8), c))
        greet(place(x, rem(y + k, 8), z, c))
    greet(place(x, block, z, 1 - c))
    for half in range(2):
        xs, zs, cs = rem(y, 4), 2 * (2 * c + half) + z_lo, div(y, 4)
        same = (xs == x) & (zs == z) & (cs == c)

        @pl.when(jnp.logical_not(same))
        def _():
            greet(place(xs, y, zs, cs))

        ys = 4 * z_lo + 2 * c + half
        same_y = (xs == x) & (ys == y) & (cs == c)

        @pl.when(jnp.logical_not(same_y))
        def _():
            greet(place(xs, ys, z, cs))

    expected = (
        21
        + jnp.where(sums_z, 4 - jnp.where(own_y, 1, 0), 0)
        + jnp.where(w_source & (c != w_core), 8, 0)
        + jnp.where(sums_y, 16 - jnp.where(part_own, 1, 0), 0)
    )

    load_cm = local(cm_hbm, cm, load_sem.at[0])
    load_rm = local(rm_hbm, rm, load_sem.at[1])
    load_cm.start()
    load_rm.start()
    own_rows = pl.ds(mul(64 + 128 * x, 64), 128)
    for q in range(NQ):
        for arr, ref in ((0, gc_hbm), (1, gr_hbm)):
            local(
                ref.at[:, LANES * q : LANES * q + LANES], gbuf.at[q, arr, c, own_rows], gload_sem.at[q]
            ).start()

    load_cm.wait()
    load_rm.wait()
    lane = lax.broadcasted_iota(jnp.int32, (128, 128), 1)
    low = lane < 64
    for j in range(4):
        middle = cm[:, 128 * j : 128 * j + 128].astype(F32)
        spread = rm[:, 128 * j : 128 * j + 128].astype(F32)
        upper = jnp.maximum(middle + spread, 0.0)
        lower = jnp.maximum(middle - spread, 0.0)
        center = (upper + lower) * 0.5
        radius = (upper - lower) * 0.5
        vsend[2 * j] = jnp.where(low, center, pltpu.roll(radius, 64, 1)).astype(BF16)
        vsend[2 * j + 1] = jnp.where(low, pltpu.roll(center, 64, 1), radius).astype(BF16)

    pl.semaphore_wait(barrier, expected)

    own_shard = z_lo * 2 + c

    def start_w(q):
        @pl.when(w_source)
        def _():
            for k in FAR:
                remote(
                    w_ref.at[q], wbuf.at[q, :, own_shard], w_send, w_recv.at[q],
                    place(x, rem(y + k, 8), z, w_core),
                ).start()

            @pl.when(c == w_core)
            def _():
                local(w_ref.at[q], wbuf.at[q, :, own_shard], w_recv.at[q]).start()

            @pl.when(c != w_core)
            def _():
                remote(
                    w_ref.at[q], wbuf.at[q, :, own_shard], w_send, w_recv.at[q], place(x, y, z, w_core)
                ).start()

    def start_g(q):
        own = gbuf.at[q, :, c, own_rows]
        bytes_of(own, gload_sem.at[q])
        for k in (2, 1, 3):
            remote(own, own, g_send, g_recv.at[q], place(rem(x + k, 4), y, z, c)).start()

    start_w(0)
    v_place = vmain.at[c, pl.ds(mul(128 * x, 128), 128)]
    for k in (2, 6, 1, 3, 5, 7, 4):
        xd, cd = rem(x + k, 4), rem(c + k // 4, 2)
        remote(vsend.at[xd + 4 * cd], v_place, v_send, v_recv, place(xd, y, z, cd)).start()
    local(vsend.at[block], v_place, v_recv).start()
    for q in range(NQ):
        if q > 0:
            start_w(q)
        start_g(q)

    zero_rows = jnp.zeros((64, LANES), BF16)

    def clear(q, _):
        for arr in range(2):
            for image in range(2):
                gbuf[q, arr, image, 0:64, :] = zero_rows
                gbuf[q, arr, image, 576:640, :] = zero_rows
        return 0

    lax.fori_loop(0, NQ, clear, 0)
    for arr in range(2):
        acc[arr] = jnp.zeros((1152, 256), F32)

    bytes_of(vmain, v_recv)
    down, up = z_hi > 0, z_hi < 3
    at_down, at_up = place(x, y, rem(z + 6, 8), c), place(x, y, rem(z + 2, 8), c)
    vh_down = remote(vmain.at[:, 0:32], vhalo.at[:, 1], vh_send.at[0], vh_recv.at[0], at_down)
    vh_up = remote(vmain.at[:, 480:512], vhalo.at[:, 0], vh_send.at[1], vh_recv.at[1], at_up)

    @pl.when(down)
    def _():
        vh_down.start()

    @pl.when(up)
    def _():
        vh_up.start()

    column = lax.broadcasted_iota(jnp.int32, (128, 128), 0) & 31

    def turn(v, piece):
        taps = (
            jnp.where(column == 0, 0.0, pltpu.roll(v, 1, 0)),
            v,
            jnp.where(column == 31, 0.0, pltpu.roll(v, 127, 0)),
        )
        for tap in range(3):
            turned = taps[tap].T.astype(BF16)
            for arr in range(2):
                vt[arr, tap * 64 : tap * 64 + 64, 128 * piece : 128 * piece + 128] = turned[
                    arr * 64 : arr * 64 + 64
                ]

    for piece in range(8):
        turn(vmain[piece // 4, 128 * (piece % 4) : 128 * (piece % 4) + 128, :].astype(F32), piece)

    ahead = rem(z_lo + c, 2) == 0
    at_mate = place(x, y, rem(jnp.where(ahead, z + 1, z + 7), 8), c)
    at_twin = place(x, y, z, 1 - c)

    def forward_g(q):
        bytes_of(gbuf.at[q, :, c, 64:448], g_recv.at[q])
        ring_rows = gbuf.at[q, :, c, 64:576]
        remote(ring_rows, ring_rows, p_send, p_recv.at[q], at_twin).start()

    def forward_w(q):
        shards = wbuf.at[q, :, pl.ds(z_lo * 2, 2)]
        bytes_of(shards, w_recv.at[q])
        remote(shards, shards, wz_send, wz_recv.at[q], at_mate).start()

    forward_g(0)
    forward_w(0)
    forward_w(1)
    @pl.when(down)
    def _():
        vh_up.wait_recv()

    @pl.when(up)
    def _():
        vh_down.wait_recv()

    @pl.when(jnp.logical_not(down))
    def _():
        vhalo[:, 0] = jnp.zeros((2, 32, 128), BF16)

    @pl.when(jnp.logical_not(up))
    def _():
        vhalo[:, 1] = jnp.zeros((2, 32, 128), BF16)

    turn(vhalo[...].astype(F32).reshape(128, 128), 8)

    def sum_of(ref):
        value = ref[0].astype(F32)
        for k in range(1, 8):
            value = value + ref[k].astype(F32)
        return value.astype(BF16)

    def reduce_first(q):
        bytes_of(rs_in.at[q], rs_recv.at[q])
        a_out[q] = sum_of(rs_in.at[q])

        @pl.when(sums_y)
        def _():
            local(a_out.at[q], a_in.at[q, y], a_recv.at[q]).start()

        @pl.when(jnp.logical_not(sums_y))
        def _():
            remote(a_out.at[q], a_in.at[q, y], a_send, a_recv.at[q], place(x, block, z, c)).start()

        bytes_of(ry_in.at[q], ry_recv.at[q])
        ay_out[q] = sum_of(ry_in.at[q])
        z_to = 2 * q + div(y, 4)

        @pl.when(z_to == z)
        def _():
            local(ay_out.at[q], ay_in.at[z], ay_recv).start()

        @pl.when(z_to != z)
        def _():
            remote(ay_out.at[q], ay_in.at[z], ay_send, ay_recv, place(x, y, z_to, c)).start()

    def reduce_last_z():
        @pl.when(sums_z)
        def _():
            bytes_of(ay_in, ay_recv)
            cy_out[...] = sum_of(ay_in)

            @pl.when(own_y)
            def _():
                local(cy_out, cy_in.at[half_y], cy_recv).start()

            @pl.when(jnp.logical_not(own_y))
            def _():
                remote(cy_out, cy_in.at[half_y], cy_send, cy_recv, place(x, block, z, core_y)).start()

            for k in range(1, 4):
                remote(
                    cy_out, cy_in.at[half_y], cy_send, cy_recv, place(rem(x + k, 4), block, z, core_y)
                ).start()

    def reduce_y(quarter):
        @pl.when(sums_y)
        def _():
            bytes_of(a_in.at[quarter], a_recv.at[quarter])
            c_out[quarter] = sum_of(a_in.at[quarter])
            z_owner = 2 * quarter + z_lo
            mine = part_own & (z_owner == z)

            @pl.when(mine)
            def _():
                local(c_out.at[quarter], c_in.at[part_half], c_recv).start()

            @pl.when(jnp.logical_not(mine))
            def _():
                remote(
                    c_out.at[quarter], c_in.at[part_half], c_send, c_recv, place(x, y, z_owner, part_core)
                ).start()

            for k in range(1, 4):
                remote(
                    c_out.at[quarter], c_in.at[part_half], c_send, c_recv,
                    place(rem(x + k, 4), y, z_owner, part_core),
                ).start()

    def gather(q):
        kern = wbuf[q].reshape(192, 3 * LANES)
        windows = []
        for arr in range(2):
            views = []
            for image in range(2):
                views.append(
                    jnp.concatenate(
                        [gbuf[q, arr, image, 96 - 32 * a : 608 - 32 * a, :] for a in range(3)], axis=1
                    )
                )
            for image in range(2):
                for first in (64, 608):
                    views.append(
                        jnp.concatenate(
                            [gbuf[q, arr, image, first - 32 * a : first + 32 - 32 * a, :] for a in range(3)],
                            axis=1,
                        )
                    )
            windows.append(jnp.concatenate(views, axis=0))
        return kern, windows

    def back(q, kern, windows):
        for arr, factor in ((0, kern), (1, jnp.abs(kern))):
            acc[arr, :, 0:192] += lax.dot_general(
                windows[arr], factor, (((1,), (1,)), ((), ())), preferred_element_type=F32
            )

    def step(q, _):
        @pl.when(q < NQ - 2)
        def _():
            forward_w(q + 2)

        bytes_of(gbuf.at[q, :, 1 - c, 64:576], p_recv.at[q])
        bytes_of(wbuf.at[q, :, pl.ds((1 - z_lo) * 2, 2)], wz_recv.at[q])
        kern, windows = gather(q)
        terms = [jnp.dot(vt[arr], windows[arr], preferred_element_type=F32) for arr in range(2)]
        wide = kern.astype(F32)
        signed = jnp.where(wide > 0, terms[1], jnp.where(wide < 0, -terms[1], 0.0))
        partial = (terms[0] + signed).astype(BF16)

        def tile(tap_at, shard):
            a, tap = divmod(tap_at, 3)
            return partial[
                tap * 64 + shard * 16 : tap * 64 + shard * 16 + 16, a * 128 : a * 128 + 128
            ]

        for to in range(8):
            for k in range(3):
                rs_out[q, to, 16 * k : 16 * k + 16, :] = tile(2 * ((to // 2) % 2) + k, (to % 2) * 2 + to // 4)
        for to in range(8):
            for k in range(2):
                ry_out[q, to, 16 * k : 16 * k + 16, :] = tile(5 + 2 * (to % 2) + k, to // 2)
        for k in FAR:
            zd, yd = rem(z + k, 8), rem(y + k, 8)
            remote(rs_out.at[q, zd], rs_in.at[q, z], rs_send, rs_recv.at[q], place(x, y, zd, c)).start()
            remote(ry_out.at[q, yd], ry_in.at[q, y], ry_send, ry_recv.at[q], place(x, yd, z, c)).start()
        local(rs_out.at[q, z], rs_in.at[q, z], rs_recv.at[q]).start()
        local(ry_out.at[q, y], ry_in.at[q, y], ry_recv.at[q]).start()

        @pl.when(q < NQ - 1)
        def _():
            forward_g(q + 1)

        back(q, kern, windows)

        @pl.when(q >= LAG)
        def _():
            reduce_first(q - LAG)

        @pl.when(q >= LAG + 1)
        def _():
            reduce_y(q - LAG - 1)
        return 0

    lax.fori_loop(0, NQ, step, 0)

    column64 = lax.broadcasted_iota(jnp.int32, (64, 128), 0) & 31
    low64 = lax.broadcasted_iota(jnp.int32, (64, 128), 1) < 64

    def fold(k, _):
        rows = pl.ds(mul(k * 64, 64), 64)
        c01, r01 = acc[0, rows, 0:128], acc[1, rows, 0:128]
        c2, r2 = acc[0, rows, 128:256], acc[1, rows, 128:256]
        first = jnp.where(low64, c01, pltpu.roll(r01, 64, 1))
        middle = jnp.where(low64, pltpu.roll(c01, 64, 1), r01)
        last = jnp.where(low64, c2, pltpu.roll(r2, 64, 1))
        value = (
            middle
            + jnp.where(column64 == 31, 0.0, pltpu.roll(first, 63, 0))
            + jnp.where(column64 == 0, 0.0, pltpu.roll(last, 1, 0))
        )
        total[rows, :] = value
        return 0

    lax.fori_loop(16, 18, fold, 0)
    for image in range(2):
        for side in range(2):
            first = 1024 + 64 * image + 32 * side
            halo_out[side, image] = total[first : first + 32, :]
    h_down = remote(halo_out.at[0], halo_in.at[0], h_send.at[0], h_recv.at[0], at_down)
    h_up = remote(halo_out.at[1], halo_in.at[1], h_send.at[1], h_recv.at[1], at_up)

    @pl.when(down)
    def _():
        h_down.start()

    @pl.when(up)
    def _():
        h_up.start()

    lax.fori_loop(0, 16, fold, 0)
    for image in range(2):
        r_out[image] = total[512 * image : 512 * image + 512, :].astype(BF16)

    def r_start(b):
        @pl.when(b == block)
        def _():
            local(r_out.at[c, pl.ds(mul(128 * x, 128), 128)], r_in.at[block], r_recv).start()

        @pl.when(b != block)
        def _():
            remote(
                r_out.at[b // 4, 128 * (b % 4) : 128 * (b % 4) + 128], r_in.at[block], r_send, r_recv,
                place(b % 4, y, z, b // 4),
            ).start()

    for b in (1, 2, 5, 6):
        r_start(b)
    for q in range(NQ - LAG, NQ):
        reduce_first(q)
        reduce_y(q - 1)

    @pl.when(up)
    def _():
        h_down.wait_recv()
        for image in range(2):
            r_out[image, 480:512, :] = (total[512 * image + 480 : 512 * image + 512, :] + halo_in[0, image]).astype(BF16)

    @pl.when(down)
    def _():
        h_up.wait_recv()
        for image in range(2):
            r_out[image, 0:32, :] = (total[512 * image : 512 * image + 32, :] + halo_in[1, image]).astype(BF16)

    for b in (0, 3, 4, 7):
        r_start(b)

    reduce_y(NQ - 1)
    reduce_last_z()

    bytes_of(r_in, r_recv)
    for j in range(4):
        lanes = slice(128 * j, 128 * j + 128)
        even, odd = r_in[2 * j].astype(F32), r_in[2 * j + 1].astype(F32)
        center = jnp.where(low, even, pltpu.roll(odd, 64, 1))
        radius = jnp.where(low, pltpu.roll(even, 64, 1), odd)
        cm_out[:, lanes], rm_out[:, lanes] = center.astype(BF16), radius.astype(BF16)

    bytes_of(vsend.at[0:7], v_send)
    bytes_of(r_in.at[0:7], r_send)

    @pl.when(down)
    def _():
        vh_down.wait_send()
        h_down.wait_send()

    @pl.when(up)
    def _():
        vh_up.wait_send()
        h_up.wait_send()

    bytes_of(gbuf.at[:, :, c, 64:448], g_send)
    bytes_of(gbuf.at[:, :, c, 64:576], p_send)
    bytes_of(wbuf.at[:, :, pl.ds(z_lo * 2, 2)], wz_send)

    @pl.when(w_source & (c == w_core))
    def _():
        bytes_of(acc.at[0, 0:1008], w_send)

    @pl.when(w_source & (c != w_core))
    def _():
        bytes_of(acc.at[0], w_send)

    bytes_of(rs_out.at[:, 0:7], rs_send)
    bytes_of(ry_out.at[:, 0:7], ry_send)

    @pl.when(jnp.logical_not(sums_y))
    def _():
        bytes_of(a_out, a_send)

    @pl.when(sums_z)
    def _():
        bytes_of(ay_out.at[0:3], ay_send)

    @pl.when(jnp.logical_not(sums_z))
    def _():
        bytes_of(ay_out, ay_send)

    @pl.when(sums_z & own_y)
    def _():
        bytes_of(ay_in.at[0:3], cy_send)

    @pl.when(sums_z & jnp.logical_not(own_y))
    def _():
        bytes_of(ay_in.at[0:4], cy_send)

    @pl.when(sums_y & part_own)
    def _():
        bytes_of(a_in.at[0:3, 0:5], c_send)

    @pl.when(sums_y & jnp.logical_not(part_own))
    def _():
        bytes_of(a_in.at[0:2], c_send)

    bytes_of(c_in, c_recv)
    bytes_of(cy_in, cy_recv)
    for rows, value in (
        ((0, 48), c_in[0]), ((48, 80), c_in[1, 16:48]), ((80, 112), cy_in[0]), ((112, 144), cy_in[1]),
    ):
        wg_out[rows[0] : rows[1], :] = value.astype(F32) * (1.0 / 32.0)


def on_device(center_mid, radius_mid, conv_weight, center_upstream, radius_upstream):
    flat = [v.reshape(128, 512) for v in (center_mid, radius_mid, center_upstream, radius_upstream)]
    weight = conv_weight.reshape(16, 3, 3, NQ, LANES).transpose(3, 2, 0, 1, 4)
    weight = weight.reshape(NQ, 3, 16, 3 * LANES)
    dma = pltpu.SemaphoreType.DMA
    hbm, vmem = pl.BlockSpec(memory_space=pltpu.HBM), pl.BlockSpec(memory_space=pltpu.VMEM)
    center_grad, radius_grad, weight_grad = pl.pallas_call(
        kernel,
        out_shape=(
            jax.ShapeDtypeStruct((128, 512), BF16),
            jax.ShapeDtypeStruct((128, 512), BF16),
            jax.ShapeDtypeStruct((144, 128), F32),
        ),
        in_specs=[hbm, hbm, hbm, hbm, vmem],
        out_specs=(vmem, vmem, vmem),
        scratch_shapes=[
            pltpu.VMEM((128, 512), BF16),
            pltpu.VMEM((128, 512), BF16),
            pltpu.VMEM((8, 128, 128), BF16),
            pltpu.VMEM((2, 512, 128), BF16),
            pltpu.VMEM((2, 2, 32, 128), BF16),
            pltpu.VMEM((2, 192, 1152), BF16),
            pltpu.VMEM((NQ, 2, 2, 640, LANES), BF16),
            pltpu.VMEM((NQ, 3, 4, 16, 3 * LANES), BF16),
            pltpu.VMEM((2, 1152, 256), F32),
            pltpu.VMEM((4, 8, 48, 128), BF16),
            pltpu.VMEM((4, 8, 48, 128), BF16),
            pltpu.VMEM((4, 8, 32, 128), BF16),
            pltpu.VMEM((4, 8, 32, 128), BF16),
            pltpu.VMEM((4, 48, 128), BF16),
            pltpu.VMEM((4, 8, 48, 128), BF16),
            pltpu.VMEM((4, 32, 128), BF16),
            pltpu.VMEM((8, 32, 128), BF16),
            pltpu.VMEM((4, 48, 128), BF16),
            pltpu.VMEM((2, 48, 128), BF16),
            pltpu.VMEM((32, 128), BF16),
            pltpu.VMEM((2, 32, 128), BF16),
            pltpu.VMEM((2, 2, 32, 128), F32),
            pltpu.VMEM((2, 2, 32, 128), F32),
            pltpu.VMEM((1152, 128), F32),
            pltpu.VMEM((2, 512, 128), BF16),
            pltpu.VMEM((8, 128, 128), BF16),
            dma((2,)), dma((NQ,)), dma, dma, dma((2,)), dma((2,)), dma, dma((NQ,)), dma, dma((NQ,)),
            dma, dma((NQ,)), dma, dma((NQ,)), dma, dma((NQ,)), dma, dma((NQ,)), dma, dma((4,)), dma, dma,
            dma, dma, dma, dma,
            dma((2,)), dma((2,)), dma, dma,
        ],
        compiler_params=pltpu.CompilerParams(
            collective_id=0, has_side_effects=True, vmem_limit_bytes=48 << 20
        ),
    )(flat[0], flat[1], flat[2], flat[3], weight)
    middle, spread = flat[0].astype(F32), flat[1].astype(F32)
    center, radius = center_grad.astype(F32), radius_grad.astype(F32)
    upper = jnp.where(middle > -spread, 0.5 * (center + radius), 0.0)
    lower = jnp.where(middle > spread, 0.5 * (center - radius), 0.0)
    center_grad, radius_grad = (upper + lower).astype(BF16), (upper - lower).astype(BF16)
    x = lax.rem(lax.axis_index("rows"), 4)
    own = lax.dynamic_slice_in_dim(weight_grad, x * 32, 32, axis=1)
    return (
        center_grad.reshape(center_mid.shape),
        radius_grad.reshape(center_mid.shape),
        own.reshape(3, 3, 16, 32).transpose(2, 0, 1, 3),
    )


def solution(mesh):
    placed = (
        P("img", "rows", None, None),
        P("img", "rows", None, None),
        P("img", None, None, None),
        P("img", "rows", None, None),
        P("img", "rows", None, None),
    )
    return jax.shard_map(
        on_device,
        mesh=mesh,
        in_specs=placed,
        out_specs=(
            P("img", "rows", None, None),
            P("img", "rows", None, None),
            P("img", None, None, "rows"),
        ),
        check_vma=False,
    )
```
